512 devices in a mesh: dp: 4 (over x), context: 16 (over z, core), tensor: 8 (over y).
Axes of the slice: x: 4, y: 8, z: 8, core: 2. Of those that a mesh axis runs over, the one named last changes fastest.
Arguments:
- xs: bfloat16 [8192, 8192], P(('dp', 'context'), 'tensor'), parts along dimension 0, may hold values from -6 to 6
- bcs: bfloat16 [8192, 2, 2048], P(('dp', 'context'), None, 'tensor'), parts along dimension 0, may hold values from -6 to 6
- zs: bfloat16 [8192, 8192], P(('dp', 'context'), 'tensor'), parts along dimension 0, may hold values from -6 to 6
- dt_raw: bfloat16 [8192, 128], P(('dp', 'context'), 'tensor'), parts along dimension 0, may hold values from -3 to 3
- tail_x: bfloat16 [12, 8192], P('dp', 'tensor'), parts along dimension 0, may hold values from -6 to 6
- tail_bc: bfloat16 [12, 2, 2048], P('dp', None, 'tensor'), parts along dimension 0, may hold values from -6 to 6
- conv_x: bfloat16 [4, 8192], P(None, 'tensor'), may hold values from -3 to 3
- conv_bc: bfloat16 [4, 2, 2048], P(None, None, 'tensor'), may hold values from -3 to 3
- dt_bias: float32 [128], P('tensor'), may hold values from -3 to -1
- a_log: float32 [128], P('tensor'), may hold values from -10 to -0.6
- d_skip: float32 [128], P('tensor'), may hold values from 0.5 to 2
- init_state: float32 [512, 64, 256], P(('dp', 'tensor')), parts along dimension 0, may hold values from -6 to 6
- norm_gain: float32 [8192], P('tensor'), may hold values from 0.5 to 1.5
- out_weight: bfloat16 [8192, 8192], P('tensor', 'context'), may hold values from -0.0625 to 0.0625
Outputs:
- mixed: bfloat16 [8192, 8192], P(('dp', 'context', 'tensor')), parts along dimension 0
The draws below stay inside these ranges and needn't reach their ends.
There are 4 independent parts, one for each index of `dp`. The reference program is written for one: setup_inputs(seed, part) draws one part's arguments, and reference() takes and returns one part's arrays. A program takes and returns all parts, laid end to end along the dimension named above; an argument that names none is the same for every part. Nothing has to cross between parts.
All inputs are finite; a program needn't handle non-finite values.
Results may differ from the reference program's by a relative error of at most 0.02.
Values may be sent and summed in bfloat16 or wider, within the bound.
No kernel may reach another device: no remote copies, remote signals or barrier semaphores. Data moves between devices by JAX's collectives and lax.ppermute only.
A program may use at most 64 MiB of HBM per device.

```python
import math
import jax
import jax.numpy as jnp
from jax import lax

D = 8192
H = 128
P_SIZE = 64
N = 256
G = 8
K = 4
DI = 8192
TOKENS = 2048
N_TENSOR = 8


def draw_a_log(key, part):
    key = jax.random.fold_in(key, 7)
    pick_key, slow_key, fast_key = jax.random.split(key, 3)
    share = 0.5
    quick = jax.random.uniform(pick_key, (H,)) < share
    slow_rate = jnp.exp(jax.random.uniform(slow_key, (H,), minval=math.log(0.3), maxval=math.log(2.0))) / (0.15 * TOKENS)
    fast_rate = jnp.exp(jax.random.uniform(fast_key, (H,), minval=math.log(0.1), maxval=math.log(0.5)))
    return jnp.log(jnp.where(quick, fast_rate, slow_rate)).astype(jnp.float32)


def block_scale(own_key, shape, cuts, smallest, top_value):
    factor_of, own = 1.0, jax.random.fold_in(own_key, 6)
    for position, shards_of in cuts:
        draws = jnp.exp(jax.random.uniform(jax.random.fold_in(own, position), (shards_of,), jnp.float32, smallest / len(cuts), top_value / len(cuts)))
        factor_of = factor_of * jnp.repeat(draws, shape[position] // shards_of).reshape([-1 if axis == position else 1 for axis in range(len(shape))])
    return factor_of


def normal_values(key, extent, spread, reach, cuts=(), kind=jnp.bfloat16):
    loudness = block_scale(key, extent, cuts, -0.22, 0.18) if cuts else 1.0
    result = jax.random.normal(key, extent, jnp.float32) * spread * loudness
    return jnp.minimum(jnp.maximum(result, -reach), reach).astype(kind)


def setup_inputs(seed: int = 0, part: int = 0) -> dict:
    keys = jax.random.split(jax.random.key(seed), 15)
    part_splits = jax.random.split(jax.random.fold_in(keys[14], part), 15)
    xs = normal_values(part_splits[0], (TOKENS, DI), 1.0, 6.0, ((0, 16), (1, 8)))
    bcs = normal_values(part_splits[1], (TOKENS, 2, G * N), 1.0, 6.0, ((0, 16), (2, 8)))
    zs = normal_values(part_splits[2], (TOKENS, DI), 1.0, 6.0, ((0, 16), (1, 8)))
    dt_raw = normal_values(part_splits[3], (TOKENS, H), 0.5, 3.0, ((0, 16), (1, 8)))
    tail_x = normal_values(part_splits[4], (K - 1, DI), 1.0, 6.0, ((1, 8),))
    tail_bc = normal_values(part_splits[5], (K - 1, 2, G * N), 1.0, 6.0, ((2, 8),))
    conv_x = normal_values(keys[6], (K, DI), K ** -0.5, 3.0, ((1, 8),))
    conv_bc = normal_values(keys[7], (K, 2, G * N), K ** -0.5, 3.0, ((2, 8),))
    dt_bias = jnp.clip(-3.0 + 2.0 * jax.random.uniform(keys[8], (H,), jnp.float32) ** block_scale(keys[8], (H,), ((0, 8),), -0.2, 0.2), -3.0, -1.0)
    a_log = draw_a_log(jax.random.fold_in(keys[14], 71), part)
    d_skip = jnp.clip(0.5 + 1.5 * jax.random.uniform(keys[10], (H,), jnp.float32) ** block_scale(keys[10], (H,), ((0, 8),), -0.2, 0.2), 0.5, 2.0)
    init_state = normal_values(part_splits[11], (H, P_SIZE, N), 1.0, 6.0, ((0, 8),), jnp.float32)
    norm_gain = jnp.clip(1.0 + 0.1 * jax.random.normal(keys[12], (DI,), jnp.float32), 0.5, 1.5)
    out_weight = normal_values(keys[13], (DI, D), DI ** -0.5, 0.0625, ((0, 8), (1, 16)))
    return dict(xs=xs, bcs=bcs, zs=zs, dt_raw=dt_raw, tail_x=tail_x, tail_bc=tail_bc, conv_x=conv_x, conv_bc=conv_bc, dt_bias=dt_bias, a_log=a_log, d_skip=d_skip, init_state=init_state, norm_gain=norm_gain, out_weight=out_weight)


def rounded(values):
    return lax.optimization_barrier(values.astype(jnp.bfloat16))

def causal_conv(prior, rows, kernel):
    full_rows = jnp.concatenate([prior.astype(jnp.float32), rows.astype(jnp.float32)], axis=0)
    length = rows.shape[0]
    running = kernel[0].astype(jnp.float32) * full_rows[0:length]
    for offset in range(1, kernel.shape[0]):
        running = running + kernel[offset].astype(jnp.float32) * full_rows[offset:offset + length]
    return rounded(jax.nn.silu(running))

def stretch_scan(inputs, deltas, rates, b_rows, c_rows, initial):
    length = inputs.shape[0]
    per_block = math.gcd(128, length)
    n_blocks = length // per_block

    def in_blocks(values):
        return values.reshape((n_blocks, per_block) + values.shape[1:])
    lower_mask = jnp.tril(jnp.ones((per_block, per_block), dtype=bool))[:, :, None, None]
    precise = lax.Precision.HIGHEST

    def advance(state, pieces):
        x_block, d_block, b_block, c_block = pieces
        cumulative = jnp.cumsum(d_block * rates, axis=0)
        spread_log = cumulative[:, None] - cumulative[None, :]
        decays = jnp.where(lower_mask, jnp.exp(jnp.where(lower_mask, spread_log, 0.0)), 0.0)
        scores = jnp.einsum('ign,jgn->ijg', c_block, b_block, precision=precise)
        weights = decays * scores[..., None] * d_block[None]
        inside = jnp.einsum('ijgh,jghc->ighc', weights, x_block, precision=precise)
        carried = jnp.einsum('ign,ghcn->ighc', c_block, state, precision=precise) * jnp.exp(cumulative)[..., None]
        trailing = jnp.exp(cumulative[-1][None] - cumulative) * d_block
        increment = jnp.einsum('jghc,jgn->ghcn', trailing[..., None] * x_block, b_block, precision=precise)
        return (jnp.exp(cumulative[-1])[..., None, None] * state + increment, inside + carried)
    final_state, outputs = lax.scan(advance, initial, (in_blocks(inputs), in_blocks(deltas), in_blocks(b_rows), in_blocks(c_rows)))
    return (outputs.reshape(inputs.shape), final_state)

def gated_norm(scan_out, gate, gain):
    gated = scan_out.astype(jnp.float32) * jax.nn.silu(gate.astype(jnp.float32))
    row_count, width = gated.shape
    grouped = gated.reshape(row_count, width // (H * P_SIZE // G), H * P_SIZE // G)
    factor = lax.rsqrt(lax.optimization_barrier(jnp.mean(grouped * grouped, axis=-1, keepdims=True)) + 1e-05)
    return ((grouped * factor).reshape(row_count, width) * gain[None, :]).astype(jnp.bfloat16)

def reference(xs, bcs, zs, dt_raw, tail_x, tail_bc, conv_x, conv_bc, dt_bias, a_log, d_skip, init_state, norm_gain, out_weight):
    x_conv = causal_conv(tail_x, xs, conv_x)
    bc_conv = causal_conv(tail_bc, bcs, conv_bc)
    length = xs.shape[0]
    per_group = H // G
    deltas = jax.nn.softplus(dt_raw.astype(jnp.float32) + dt_bias[None, :]).reshape(length, G, per_group)
    rates = (-jnp.exp(a_log)).reshape(G, per_group)
    inputs = x_conv.astype(jnp.float32).reshape(length, G, per_group, P_SIZE)
    bc_wide = bc_conv.astype(jnp.float32).reshape(length, 2, G, N)
    initial = init_state.reshape(G, per_group, P_SIZE, N)
    outputs, final_state = stretch_scan(inputs, deltas, rates, bc_wide[:, 0], bc_wide[:, 1], initial)
    skips = d_skip.reshape(G, per_group)[None, :, :, None]
    scan_out = (outputs + skips * inputs).astype(jnp.bfloat16).reshape(length, H * P_SIZE)
    normed = gated_norm(scan_out, zs, norm_gain)
    part_width = H * P_SIZE // N_TENSOR
    summed = jnp.zeros((length, out_weight.shape[1]), jnp.float32)
    for shard_index in range(N_TENSOR):
        lo_row = shard_index * part_width
        block_part = jnp.dot(normed[:, lo_row:lo_row + part_width], out_weight[lo_row:lo_row + part_width], preferred_element_type=jnp.float32)
        summed = summed + rounded(block_part).astype(jnp.float32)
    return summed.astype(jnp.bfloat16)
```

```python
import jax
import jax.numpy as jnp
from jax import lax
from jax.experimental import pallas as pl
from jax.experimental.pallas import tpu as pltpu
from jax.sharding import PartitionSpec as P

ROWS = 128
CHIP = 256
HALF = 512
HEADS = 8
P_SIZE = 64
N = 256
CHIPS = 8
PAIR = [(i, i ^ 1) for i in range(16)]
SAME_CORE = [[2 * i + k for i in range(CHIPS)] for k in range(2)]
CHIP_PAIRS = [[4 * q + i for i in range(4)] for q in range(4)]
STRIDED = [[4 * i + 2 * b + k for i in range(4)] for b in range(2) for k in range(2)]
UP = [(i, (i + 4) % 16) for i in range(16)]
DOWN = [(i, (i - 4) % 16) for i in range(16)]
TO_CORE_0 = [(2 * i + 1, 2 * i + 2) for i in range(CHIPS - 1)]
TO_CORE_1 = [(2 * i + 1, 2 * i + 3) for i in range(CHIPS - 1)]
F32 = jnp.float32
BF16 = jnp.bfloat16
EXACT = lax.Precision.HIGHEST
LIMIT = 40 * 1024 * 1024


def call(kernel, out_shape, scratch=(), flops=0, moved=0, **kwargs):
    return pl.pallas_call(
        kernel,
        out_shape=out_shape,
        scratch_shapes=list(scratch),
        compiler_params=pltpu.CompilerParams(vmem_limit_bytes=LIMIT),
        cost_estimate=pl.CostEstimate(flops=flops, bytes_accessed=moved, transcendentals=0),
        **kwargs,
    )


SMEM = pl.BlockSpec(memory_space=pltpu.SMEM)
VMEM = pl.BlockSpec(memory_space=pltpu.VMEM)


def shaped(shape, dtype):
    return jax.ShapeDtypeStruct(shape, dtype)


def silu(v):
    return v / (1.0 + jnp.exp(-v))


def half_of(ref, core):
    return ref[:, pl.ds(pl.multiple_of(core * HALF, HALF), HALF)]


def spread():
    head = lax.broadcasted_iota(jnp.int32, (128, HALF), 0)
    lane = lax.broadcasted_iota(jnp.int32, (128, HALF), 1)
    return (lane // P_SIZE == head).astype(F32)


def pack_kernel(where, xs, zs, bc, dt_other, send, halo_0, halo_1):
    core = where[0]
    send[:, 0:512] = half_of(xs, 1 - core)
    send[:, 512:1024] = half_of(zs, 1 - core)
    send[:, 1024:1536] = bc[...]
    send[:, 1536:1664] = dt_other[...]
    halo_0[:, 0:512] = xs[112:128, 0:512]
    halo_0[:, 512:1024] = bc[112:128, :]
    halo_1[:, 0:512] = xs[112:128, 512:1024]
    halo_1[:, 512:1024] = bc[112:128, :]


def conv_kernel(
    where, xs, bc, dt_own, got, halo_0, halo_1, tail, taps, heads,
    x_out, bc_out, cum_out, delta_out, send, rows, steps,
):
    core, chip = where[0], where[1]
    mine = pl.multiple_of(core * ROWS, ROWS)
    other = pl.multiple_of((1 - core) * ROWS, ROWS)
    rows[pl.ds(16 + mine, ROWS), 0:512] = half_of(xs, core).astype(F32)
    rows[pl.ds(16 + mine, ROWS), 512:1024] = bc[...].astype(F32)
    rows[pl.ds(16 + other, ROWS), 0:512] = got[:, 0:512].astype(F32)
    rows[pl.ds(16 + other, ROWS), 512:1024] = got[:, 1024:1536].astype(F32)
    halo = halo_0[...].astype(F32) + halo_1[...].astype(F32)
    rows[0:16, :] = jnp.where(chip == 0, tail[...], halo)
    for lane in range(0, 1024, 128):
        cut = slice(lane, lane + 128)
        total = taps[0:1, cut] * rows[13 : 13 + CHIP, cut]
        for k in range(1, 4):
            total = total + taps[k : k + 1, cut] * rows[13 + k : 13 + k + CHIP, cut]
        value = silu(total).astype(BF16)
        if lane < 512:
            x_out[:, cut] = value
        else:
            bc_out[:, lane - 512 : lane - 384] = value
    steps[pl.ds(mine, ROWS), :] = dt_own[...].astype(F32)
    steps[pl.ds(other, ROWS), :] = got[:, 1536:1664].astype(F32)
    raw = steps[...] + heads[0:1, 0:128]
    delta = jnp.maximum(raw, 0.0) + jnp.log(1.0 + jnp.exp(-jnp.abs(raw)))
    logs = delta * -jnp.exp(heads[1:2, 0:128])
    row = lax.broadcasted_iota(jnp.int32, (CHIP, CHIP), 0)
    column = lax.broadcasted_iota(jnp.int32, (CHIP, CHIP), 1)
    cum = jnp.dot((row >= column).astype(F32), logs, precision=EXACT, preferred_element_type=F32)
    cum_out[...] = cum
    delta_out[...] = delta
    last = cum[CHIP - 1 : CHIP, :]
    trailing = jnp.dot(jnp.exp(last - cum) * delta, spread(), precision=EXACT, preferred_element_type=F32)
    weighted = (x_out[...].astype(F32) * trailing).astype(BF16)
    added = lax.dot_general(
        weighted, bc_out[:, 0:N], (((0,), (0,)), ((), ())), preferred_element_type=F32
    )
    high = last.astype(BF16).astype(F32)
    middle = (last - high).astype(BF16).astype(F32)
    low = last - high - middle
    line = lax.broadcasted_iota(jnp.int32, (16, N), 0)
    for h in range(HEADS):
        send[h, 0:P_SIZE, :] = added[h * P_SIZE : (h + 1) * P_SIZE].astype(BF16)
        terms = jnp.where(
            line == 0,
            jnp.broadcast_to(high[:, h : h + 1], (16, N)),
            jnp.where(
                line == 1,
                jnp.broadcast_to(middle[:, h : h + 1], (16, N)),
                jnp.where(line == 2, jnp.broadcast_to(low[:, h : h + 1], (16, N)), 0.0),
            ),
        )
        send[h, P_SIZE : P_SIZE + 16, :] = terms.astype(BF16)


def inside_kernel(x, bc, cum, delta, heads, out):
    scores = lax.dot_general(
        bc[:, N : 2 * N], bc[:, 0:N], (((1,), (1,)), ((), ())), preferred_element_type=F32
    )
    row = lax.broadcasted_iota(jnp.int32, (CHIP, CHIP), 0)
    column = lax.broadcasted_iota(jnp.int32, (CHIP, CHIP), 1)
    scores = jnp.where(row >= column, scores, 0.0)
    cum_t = jnp.transpose(cum[...])
    delta_t = jnp.transpose(delta[...])
    lane = lax.broadcasted_iota(jnp.int32, (CHIP, 128), 1)
    for pair in range(HEADS // 2):
        cut = slice(pair * 128, pair * 128 + 128)
        values = x[:, cut]
        both = []
        for h in (2 * pair, 2 * pair + 1):
            decay = jnp.exp(jnp.minimum(cum[:, h : h + 1] - cum_t[h : h + 1, :], 0.0))
            weights = (decay * scores * delta_t[h : h + 1, :]).astype(BF16)
            both.append(jnp.dot(weights, values, preferred_element_type=F32))
        out[:, cut] = jnp.where(lane < P_SIZE, both[0], both[1]) + heads[2:3, cut] * values.astype(F32)


def prefix_kernel(got, first, out):
    state = first[...]
    for chip in range(CHIPS):
        out[chip] = state.astype(BF16)
        if chip < CHIPS - 1:
            terms = got[chip, P_SIZE : P_SIZE + 16, :].astype(F32)
            decay = jnp.exp(terms[0:1] + terms[1:2] + terms[2:3])
            state = decay * state + got[chip, 0:P_SIZE, :].astype(F32)


def gate_kernel(where, state, bc, cum, inside, zs, got, keep, send, total):
    core = where[0]
    mine = pl.multiple_of(core * ROWS, ROWS)
    other = pl.multiple_of((1 - core) * ROWS, ROWS)
    carried = lax.dot_general(
        bc[:, N : 2 * N], state[...], (((1,), (1,)), ((), ())), preferred_element_type=F32
    )
    decay = jnp.dot(jnp.exp(cum[...]), spread(), precision=EXACT, preferred_element_type=F32)
    total[...] = inside[...] + carried * decay
    keep[...] = total[pl.ds(mine, ROWS), :] * silu(half_of(zs, core).astype(F32))
    send[...] = (total[pl.ds(other, ROWS), :] * silu(got[:, 512:1024].astype(F32))).astype(BF16)


def norm_kernel(where, keep, got, gain, out):
    core = where[0]
    own, came = keep[...], got[...].astype(F32)
    squares = jnp.sum(own * own + came * came, axis=1, keepdims=True)
    factor = lax.rsqrt(squares * (1.0 / 1024.0) + 1e-05)
    at_own = pl.ds(pl.multiple_of(core * HALF, HALF), HALF)
    at_came = pl.ds(pl.multiple_of((1 - core) * HALF, HALF), HALF)
    out[:, at_own] = (own * factor * gain[:, at_own]).astype(BF16)
    out[:, at_came] = (came * factor * gain[:, at_came]).astype(BF16)


def product_kernel(where, own, below, above, far_low, far_high, weight, out):
    place = where[1] // 2

    def put(rows, block, first, count):
        value = jnp.dot(rows, weight[0], preferred_element_type=F32).astype(BF16)
        out[first : first + count, pl.ds(block, 1), :, :] = value.reshape(count, 1, 16, 512)

    put(own[...], place, 0, 8)
    put(below[...], (place + 3) % 4, 0, 8)
    put(above[...], (place + 1) % 4, 0, 8)
    put(far_low[...], (place + 2) % 4, 0, 4)
    put(far_high[...], (place + 2) % 4, 4, 4)


def body(
    xs, bcs, zs, dt_raw, tail_x, tail_bc, conv_x, conv_bc,
    dt_bias, a_log, d_skip, init_state, norm_gain, out_weight,
):
    position = lax.axis_index("context")
    core, chip = position % 2, position // 2
    where = jnp.stack([core, chip]).astype(jnp.int32)

    weights = lax.all_gather(
        out_weight, "context", axis=0, tiled=True, axis_index_groups=CHIP_PAIRS
    ).reshape(4, 1024, 512)

    bc = bcs.reshape(ROWS, 512)

    def steps_of(side):
        return jnp.pad(lax.dynamic_slice_in_dim(dt_raw, side * HEADS, HEADS, 1), ((0, 0), (0, 120)))

    send, halo_0, halo_1 = call(
        pack_kernel,
        (shaped((ROWS, 1664), BF16), shaped((16, 1024), BF16), shaped((16, 1024), BF16)),
        in_specs=[SMEM, VMEM, VMEM, VMEM, VMEM],
        moved=1 << 20,
    )(where, xs, zs, bc, steps_of(1 - core))
    got = lax.ppermute(send, "context", PAIR)
    halo_0 = lax.ppermute(halo_0, "context", TO_CORE_0)
    halo_1 = lax.ppermute(halo_1, "context", TO_CORE_1)

    def own_channels(value):
        return lax.dynamic_slice_in_dim(value, core * HALF, HALF, 1).astype(F32)

    def own_heads(value):
        return lax.dynamic_slice_in_dim(value, core * HEADS, HEADS, 0)

    tail = jnp.pad(
        jnp.concatenate([own_channels(tail_x), tail_bc.reshape(3, 512).astype(F32)], axis=1), ((13, 0), (0, 0))
    )
    taps = jnp.concatenate([own_channels(conv_x), conv_bc.reshape(4, 512).astype(F32)], axis=1)
    heads = jnp.stack(
        [
            jnp.pad(own_heads(dt_bias), (0, HALF - HEADS)),
            jnp.pad(own_heads(a_log), (0, HALF - HEADS)),
            jnp.repeat(own_heads(d_skip), P_SIZE),
        ]
    )
    x_conv, bc_conv, cum, delta, added = call(
        conv_kernel,
        (
            shaped((CHIP, HALF), BF16),
            shaped((CHIP, 512), BF16),
            shaped((CHIP, 128), F32),
            shaped((CHIP, 128), F32),
            shaped((HEADS, P_SIZE + 16, N), BF16),
        ),
        scratch=[pltpu.VMEM((CHIP + 16, 1024), F32), pltpu.VMEM((CHIP, 128), F32)],
        in_specs=[SMEM] + [VMEM] * 9,
        flops=200_000_000,
        moved=2 << 20,
    )(where, xs, bc, steps_of(core), got, halo_0, halo_1, tail, taps, heads)
    increments = lax.all_to_all(added, "context", 0, 0, tiled=True, axis_index_groups=SAME_CORE)
    inside = call(
        inside_kernel,
        shaped((CHIP, HALF), F32),
        in_specs=[VMEM] * 5,
        flops=400_000_000,
        moved=2 << 20,
    )(x_conv, bc_conv, cum, delta, heads)
    first = lax.dynamic_index_in_dim(init_state, core * HEADS + chip, 0, keepdims=False)
    states = call(
        prefix_kernel,
        shaped((CHIPS, P_SIZE, N), BF16),
        in_specs=[VMEM] * 2,
        moved=1 << 20,
    )(increments, first)
    states = lax.all_to_all(states, "context", 0, 0, tiled=True, axis_index_groups=SAME_CORE)
    keep, give = call(
        gate_kernel,
        (shaped((ROWS, HALF), F32), shaped((ROWS, HALF), BF16)),
        scratch=[pltpu.VMEM((CHIP, HALF), F32)],
        in_specs=[SMEM] + [VMEM] * 6,
        flops=100_000_000,
        moved=2 << 20,
    )(where, states.reshape(HEADS * P_SIZE, N), bc_conv, cum, inside, zs, got)
    came = lax.ppermute(give, "context", PAIR)
    normed = call(
        norm_kernel,
        shaped((ROWS, 1024), BF16),
        in_specs=[SMEM] + [VMEM] * 3,
        moved=1 << 20,
    )(where, keep, came, norm_gain.reshape(1, 1024))

    below = lax.ppermute(normed, "context", UP)
    above = lax.ppermute(normed, "context", DOWN)
    far_low = lax.ppermute(below[:64], "context", UP)
    far_high = lax.ppermute(above[64:], "context", DOWN)
    whole = lambda rows: pl.BlockSpec((rows, 1024), lambda j: (0, 0))
    partial_sums = call(
        product_kernel,
        shaped((8, 4, 16, 2048), BF16),
        grid=(4,),
        in_specs=[
            SMEM, whole(128), whole(128), whole(128), whole(64), whole(64),
            pl.BlockSpec((1, 1024, 512), lambda j: (j, 0, 0)),
        ],
        out_specs=pl.BlockSpec((8, 4, 16, 512), lambda j: (0, 0, 0, j)),
        flops=2_200_000_000,
        moved=7 << 20,
    )(where, normed, below, above, far_low, far_high, weights)
    summed = lax.psum_scatter(
        partial_sums.reshape(512, 2048), "tensor", scatter_dimension=0, tiled=True
    )
    return lax.all_to_all(
        summed.reshape(4, 16, 2048), "context", 0, 0, tiled=True, axis_index_groups=STRIDED
    ).transpose(1, 0, 2).reshape(16, 8192)


def solution(mesh):
    return jax.shard_map(
        body,
        mesh=mesh,
        in_specs=(
            P(("dp", "context"), "tensor"),
            P(("dp", "context"), None, "tensor"),
            P(("dp", "context"), "tensor"),
            P(("dp", "context"), "tensor"),
            P("dp", "tensor"),
            P("dp", None, "tensor"),
            P(None, "tensor"),
            P(None, None, "tensor"),
            P("tensor"),
            P("tensor"),
            P("tensor"),
            P(("dp", "tensor"), None, None),
            P("tensor"),
            P("tensor", "context"),
        ),
        out_specs=P(("dp", "context", "tensor"), None),
        check_vma=False,
    )
```

```python
import functools

import jax
import jax.numpy as jnp
from jax import lax
from jax.experimental import pallas as pl
from jax.experimental.pallas import tpu as pltpu
from jax.sharding import PartitionSpec as P

ROWS = 128
CHIP = 256
HALF = 512
HEADS = 8
P_SIZE = 64
N = 256
CHIPS = 8
PAIR = [(i, i ^ 1) for i in range(16)]
SAME_CORE = [[2 * i + k for i in range(CHIPS)] for k in range(2)]
UP = [(i, (i + 2) % 16) for i in range(16)]
DOWN = [(i, (i - 2) % 16) for i in range(16)]
CROSS = [(8 * i + t, 8 * (i ^ 1) + (t ^ 1)) for i in range(16) for t in range(8)]
BESIDE = [(t, t ^ 1) for t in range(8)]
PARITY = [[0, 2, 4, 6], [1, 3, 5, 7]]
CORES = [[2 * i, 2 * i + 1] for i in range(CHIPS)]
BOTH = [[0, 1], [2, 3], [4, 5], [6, 7]]
NEAR = (0, 1, 7, 2, 6)
FAR = (3, 5, 4)
TO_CORE_0 = [(2 * i + 1, 2 * i + 2) for i in range(CHIPS - 1)]
TO_CORE_1 = [(2 * i + 1, 2 * i + 3) for i in range(CHIPS - 1)]
F32 = jnp.float32
BF16 = jnp.bfloat16
EXACT = lax.Precision.HIGHEST
LIMIT = 24 * 1024 * 1024
WIDE = 63 * 1024 * 1024


def call(kernel, out_shape, scratch=(), flops=0, moved=0, limit=LIMIT, **kwargs):
    return pl.pallas_call(
        kernel,
        out_shape=out_shape,
        scratch_shapes=list(scratch),
        compiler_params=pltpu.CompilerParams(vmem_limit_bytes=limit),
        cost_estimate=pl.CostEstimate(flops=flops, bytes_accessed=moved, transcendentals=0),
        **kwargs,
    )


SMEM = pl.BlockSpec(memory_space=pltpu.SMEM)
VMEM = pl.BlockSpec(memory_space=pltpu.VMEM)
HBM = pl.BlockSpec(memory_space=pltpu.HBM)


def shaped(shape, dtype):
    return jax.ShapeDtypeStruct(shape, dtype)


def silu(v):
    return v / (1.0 + jnp.exp(-v))


def half_of(ref, core):
    return ref[:, pl.ds(pl.multiple_of(core * HALF, HALF), HALF)]


def spread():
    head = lax.broadcasted_iota(jnp.int32, (128, HALF), 0)
    lane = lax.broadcasted_iota(jnp.int32, (128, HALF), 1)
    return (lane // P_SIZE == head).astype(F32)


def place():
    position = lax.axis_index("context")
    return lax.rem(position, 2), lax.div(position, 2)


def copies(pairs, sems):
    return [pltpu.make_async_copy(source, target, sems.at[i]) for i, (source, target) in enumerate(pairs)]


def fetch(pairs, sems):
    moving = copies(pairs, sems)
    for copy in moving:
        copy.start()
    for copy in moving:
        copy.wait()


def lanes(core):
    return pl.ds(pl.multiple_of(core * HALF, HALF), HALF)


def tokens(core):
    return pl.ds(pl.multiple_of(core * ROWS, ROWS), ROWS)


TAPS, BIAS, RATE = 16, 20, 21


def pack_kernel(
    xs, zs, bcs, dt, tail_x, tail_bc, taps_x, taps_bc, bias, rate,
    send, halo_0, halo_1, mine, fixed, b_c, steps, tail_2, tail_3, taps_2, taps_3, bias_1, rate_1, heads, sems,
):
    core, _ = place()
    heads[...] = jnp.zeros((2, 128), F32)
    fetch(
        [
            (bcs, b_c),
            (dt, steps),
            (tail_x, tail_2),
            (tail_bc, tail_3),
            (taps_x, taps_2),
            (taps_bc, taps_3),
            (bias, bias_1),
            (rate, rate_1),
            (xs.at[:, lanes(1 - core)], send.at[:, 0:512]),
            (zs.at[:, lanes(1 - core)], send.at[:, 1152:1664]),
            (xs.at[:, lanes(core)], mine),
            (xs.at[112:128, 0:512], halo_0.at[:, 0:512]),
            (xs.at[112:128, 512:1024], halo_1.at[:, 0:512]),
        ],
        sems,
    )
    send[:, 512:768] = b_c[:, 0, :]
    send[:, 768:1024] = b_c[:, 1, :]
    by_head = jnp.concatenate([steps[...].astype(F32), jnp.zeros((112, ROWS), F32)], axis=0)
    send[:, 1024:1152] = jnp.transpose(by_head).astype(BF16)
    halo_0[:, 512:1024] = send[112:128, 512:1024]
    halo_1[:, 512:1024] = send[112:128, 512:1024]
    fixed[...] = jnp.zeros((32, 1024), F32)
    fixed[13:16, 0:512] = half_of(tail_2, core).astype(F32)
    fixed[13:16, 512:768] = tail_3[:, 0, :].astype(F32)
    fixed[13:16, 768:1024] = tail_3[:, 1, :].astype(F32)
    fixed[TAPS : TAPS + 4, 0:512] = half_of(taps_2, core).astype(F32)
    fixed[TAPS : TAPS + 4, 512:768] = taps_3[:, 0, :].astype(F32)
    fixed[TAPS : TAPS + 4, 768:1024] = taps_3[:, 1, :].astype(F32)
    heads[0:1, 0:16] = bias_1[...]
    heads[1:2, 0:16] = rate_1[...]
    own = jnp.where(core == 0, heads[...], pltpu.roll(heads[...], 120, 1))
    fixed[BIAS : BIAS + 1, 0:128] = own[0:1]
    fixed[RATE : RATE + 1, 0:128] = -jnp.exp(own[1:2])


def conv_kernel(
    xs_in, sent_in, got_in, halo_0_in, halo_1_in, fixed_in,
    added_out, x_out, bc_out, cum_out, delta_out, rows, steps, x_conv, bc_conv, cums, deltas,
    xs, sent, got, halo_0, halo_1, fixed, sems,
):
    core, chip = place()
    mine, other = tokens(core), tokens(1 - core)
    fetch(
        [
            (xs_in, xs),
            (sent_in.at[:, 512:1152], sent),
            (got_in.at[:, 0:1152], got),
            (halo_0_in, halo_0),
            (halo_1_in, halo_1),
            (fixed_in, fixed),
        ],
        sems.at[4:10],
    )
    first = pl.multiple_of(core * ROWS + 16, 16)
    second = pl.multiple_of((1 - core) * ROWS + 16, 16)
    rows[pl.ds(first, ROWS), 0:512] = xs[...].astype(F32)
    rows[pl.ds(first, ROWS), 512:1024] = sent[:, 0:512].astype(F32)
    rows[pl.ds(second, ROWS), :] = got[:, 0:1024].astype(F32)
    halo = halo_0[...].astype(F32) + halo_1[...].astype(F32)
    rows[0:16, :] = jnp.where(chip == 0, fixed[0:16, :], halo)
    for lane in range(0, 1024, 128):
        cut = slice(lane, lane + 128)
        total = fixed[TAPS : TAPS + 1, cut] * rows[13 : 13 + CHIP, cut]
        for k in range(1, 4):
            total = total + fixed[TAPS + k : TAPS + k + 1, cut] * rows[13 + k : 13 + k + CHIP, cut]
        value = silu(total).astype(BF16)
        if lane < 512:
            x_conv[:, cut] = value
        else:
            bc_conv[:, lane - 512 : lane - 384] = value
    steps[mine, :] = sent[:, 512:640].astype(F32)
    steps[other, :] = got[:, 1024:1152].astype(F32)
    raw = jnp.where(core == 0, steps[...], pltpu.roll(steps[...], 120, 1)) + fixed[BIAS : BIAS + 1, 0:128]
    delta = jnp.maximum(raw, 0.0) + jnp.log(1.0 + jnp.exp(-jnp.abs(raw)))
    logs = delta * fixed[RATE : RATE + 1, 0:128]
    row = lax.broadcasted_iota(jnp.int32, (CHIP, CHIP), 0)
    column = lax.broadcasted_iota(jnp.int32, (CHIP, CHIP), 1)
    cum = jnp.dot((row >= column).astype(F32), logs, precision=EXACT, preferred_element_type=F32)
    cums[...] = cum
    deltas[...] = delta
    kept = copies(
        [(x_conv, x_out), (bc_conv, bc_out), (cums, cum_out), (deltas, delta_out)],
        sems.at[0:4],
    )
    for copy in kept:
        copy.start()
    last = cum[CHIP - 1 : CHIP, :]
    trailing = jnp.dot(jnp.exp(last - cum) * delta, spread(), precision=EXACT, preferred_element_type=F32)
    weighted = (x_conv[...].astype(F32) * trailing).astype(BF16)
    added = lax.dot_general(
        weighted, bc_conv[:, 0:N], (((0,), (0,)), ((), ())), preferred_element_type=F32
    )
    high = last.astype(BF16).astype(F32)
    middle = (last - high).astype(BF16).astype(F32)
    low = last - high - middle
    line = lax.broadcasted_iota(jnp.int32, (16, N), 0)
    for h in range(HEADS):
        added_out[h, 0:P_SIZE, :] = added[h * P_SIZE : (h + 1) * P_SIZE].astype(BF16)
        terms = jnp.where(
            line == 0,
            jnp.broadcast_to(high[:, h : h + 1], (16, N)),
            jnp.where(
                line == 1,
                jnp.broadcast_to(middle[:, h : h + 1], (16, N)),
                jnp.where(line == 2, jnp.broadcast_to(low[:, h : h + 1], (16, N)), 0.0),
            ),
        )
        added_out[h, P_SIZE : P_SIZE + 16, :] = terms.astype(BF16)
    for copy in kept:
        copy.wait()


def inside_kernel(x_in, bc_in, cum_in, delta_in, skip, out, x, bc, cum, delta, total, sems):
    core, _ = place()
    fetch([(x_in, x), (bc_in, bc), (cum_in, cum), (delta_in, delta)], sems)
    scores = lax.dot_general(
        bc[:, N : 2 * N], bc[:, 0:N], (((1,), (1,)), ((), ())), preferred_element_type=F32
    )
    row = lax.broadcasted_iota(jnp.int32, (CHIP, CHIP), 0)
    column = lax.broadcasted_iota(jnp.int32, (CHIP, CHIP), 1)
    scores = jnp.where(row >= column, scores, 0.0)
    cum_t = jnp.transpose(cum[...])
    delta_t = jnp.transpose(delta[...])
    lane = lax.broadcasted_iota(jnp.int32, (CHIP, 128), 1)
    for pair in range(HEADS // 2):
        cut = slice(pair * 128, pair * 128 + 128)
        values = x[:, cut]
        both = []
        for h in (2 * pair, 2 * pair + 1):
            decay = jnp.exp(jnp.minimum(cum[:, h : h + 1] - cum_t[h : h + 1, :], 0.0))
            weights = (decay * scores * delta_t[h : h + 1, :]).astype(BF16)
            through = skip[core * HEADS + h] * values.astype(F32)
            both.append(jnp.dot(weights, values, preferred_element_type=F32) + through)
        total[:, cut] = jnp.where(lane < P_SIZE, both[0], both[1])
    fetch([(total, out)], sems)


def prefix_kernel(got, first, out):
    state = first[...]
    for chip in range(CHIPS):
        out[chip] = state.astype(BF16)
        if chip < CHIPS - 1:
            terms = got[chip, P_SIZE : P_SIZE + 16, :].astype(F32)
            decay = jnp.exp(terms[0:1] + terms[1:2] + terms[2:3])
            state = decay * state + got[chip, 0:P_SIZE, :].astype(F32)


def carry_kernel(
    state_in, bc_in, cum_in, inside_in, zs, got, gain_in,
    keep, to_core, to_next, to_cross, state, c, cum, inside, gate, gain, pieces, sems,
):
    core, _ = place()
    fetch(
        [
            (bc_in.at[:, N : 2 * N], c),
            (cum_in, cum),
            (inside_in, inside),
            (zs.at[:, lanes(core)], gate.at[tokens(core), :]),
            (got.at[:, 1152:1664], gate.at[tokens(1 - core), :]),
            (state_in, state),
            (gain_in, gain),
        ],
        sems,
    )
    carried = lax.dot_general(
        c[...], state[...], (((1,), (1,)), ((), ())), preferred_element_type=F32
    )
    decay = jnp.dot(jnp.exp(cum[...]), spread(), precision=EXACT, preferred_element_type=F32)
    gated = (inside[...] + carried * decay) * silu(gate[...].astype(F32))
    pieces[...] = gated.astype(BF16).reshape(2, 4, 2, 16, HALF)

    def piece(side, parity):
        return pieces[pl.ds(side, 1), :, pl.ds(parity, 1)].reshape(64, HALF)

    odd = lax.rem(lax.axis_index("tensor"), 2)
    whole = gain[:, lanes(core)]
    high = whole.astype(BF16).astype(F32)
    middle = (whole - high).astype(BF16).astype(F32)
    low = whole - high - middle
    line = lax.broadcasted_iota(jnp.int32, (16, HALF), 0)
    terms = jnp.where(line == 0, high, jnp.where(line == 1, middle, jnp.where(line == 2, low, 0.0)))
    for out, side, parity in (
        (keep, core, odd), (to_core, 1 - core, odd), (to_next, core, 1 - odd), (to_cross, 1 - core, 1 - odd),
    ):
        out[0:64, :] = piece(side, parity)
        out[64:80, :] = terms.astype(BF16)


def norm_kernel(keep, core_got, next_got, cross_got, out):
    core, _ = place()
    odd = lax.rem(lax.axis_index("tensor"), 2)
    for mine, came, position in ((keep, core_got, odd), (next_got, cross_got, 1 - odd)):
        values = [ref[0:64, :].astype(F32) for ref in (mine, came)]
        squares = jnp.sum(values[0] * values[0] + values[1] * values[1], axis=1, keepdims=True)
        factor = lax.rsqrt(squares * (1.0 / 1024.0) + 1e-05)
        for ref, value, side in ((mine, values[0], core), (came, values[1], 1 - core)):
            terms = ref[64:80, :].astype(F32)
            gain = terms[0:1] + terms[1:2] + terms[2:3]
            at = pl.ds(pl.multiple_of(position * 1024 + side * HALF, HALF), HALF)
            out[:, at] = (value * factor * gain).astype(BF16)


def product_kernel(*refs):
    *blocks, weights_in, out, rows, weights, result, sems = refs
    count = len(blocks)
    weight_copies = copies([(weights_in.at[i], weights.at[i]) for i in range(4)], sems)
    row_copies = copies([(block, rows.at[r * 64 : (r + 1) * 64]) for r, block in enumerate(blocks)], sems.at[4:])
    for copy in weight_copies[:1] + row_copies + weight_copies[1:]:
        copy.start()
    for copy in row_copies:
        copy.wait()
    moving = []
    for side in range(2):
        weight_copies[2 * side].wait()
        value = jnp.dot(rows[:, 0:1024], weights[2 * side], preferred_element_type=F32)
        weight_copies[2 * side + 1].wait()
        value = value + jnp.dot(rows[:, 1024:2048], weights[2 * side + 1], preferred_element_type=F32)
        value = value.astype(BF16)
        for r in range(count):
            result[side, :, r] = value[r * 64 : (r + 1) * 64].reshape(4, 16, HALF)
        copy = pltpu.make_async_copy(
            result.at[side], out.at[:, :, :, side * HALF : (side + 1) * HALF], sems.at[4 + count + side]
        )
        copy.start()
        moving.append(copy)
    for copy in moving:
        copy.wait()


def product(blocks, weights):
    count = len(blocks)
    return call(
        product_kernel,
        shaped((4, count, 16, 1024), BF16),
        scratch=[
            pltpu.VMEM((count * 64, 2048), BF16),
            pltpu.VMEM((4, 1024, HALF), BF16),
            pltpu.VMEM((2, 4, count, 16, HALF), BF16),
            pltpu.SemaphoreType.DMA((6 + count,)),
        ],
        in_specs=[HBM] * (count + 1),
        out_specs=HBM,
        limit=WIDE,
    )(*blocks, weights)


def summed_over(terms, unit):
    total = terms[0, unit].astype(F32)
    for source in range(1, 4):
        total = total + terms[source, unit].astype(F32)
    return total.astype(BF16)


def collect_kernel(near, far, out, summed, sems):
    _, chip = place()
    moving = copies([(near, summed)], sems)
    moving[0].start()
    for r, before in enumerate(FAR):
        out[lax.rem(chip + (CHIPS - before), CHIPS)] = summed_over(far, r)
    moving[0].wait()
    for r, before in enumerate(NEAR):
        out[lax.rem(chip + (CHIPS - before), CHIPS)] = summed[r]


def body(
    xs, bcs, zs, dt_raw, tail_x, tail_bc, conv_x, conv_bc,
    dt_bias, a_log, d_skip, init_state, norm_gain, out_weight,
):
    core, chip = place()
    weights = lax.all_gather(out_weight, "tensor", axis=0, tiled=True, axis_index_groups=BOTH)
    sent, halo_0, halo_1, mine, fixed = call(
        pack_kernel,
        (
            shaped((ROWS, 1664), BF16),
            shaped((16, 1024), BF16),
            shaped((16, 1024), BF16),
            shaped((ROWS, HALF), BF16),
            shaped((32, 1024), F32),
        ),
        scratch=[
            pltpu.VMEM((ROWS, 2, N), BF16),
            pltpu.VMEM((16, ROWS), BF16),
            pltpu.VMEM((3, 1024), BF16),
            pltpu.VMEM((3, 2, N), BF16),
            pltpu.VMEM((4, 1024), BF16),
            pltpu.VMEM((4, 2, N), BF16),
            pltpu.VMEM((1, 16), F32),
            pltpu.VMEM((1, 16), F32),
            pltpu.VMEM((2, 128), F32),
            pltpu.SemaphoreType.DMA((13,)),
        ],
        in_specs=[HBM] * 10,
        out_specs=[VMEM] * 5,
        moved=1 << 20,
        limit=WIDE,
    )(
        xs, zs, bcs, dt_raw.T, tail_x, tail_bc, conv_x, conv_bc,
        dt_bias.reshape(1, 16), a_log.reshape(1, 16),
    )
    got = lax.ppermute(sent, "context", PAIR)
    halo_0 = lax.ppermute(halo_0, "context", TO_CORE_0)
    halo_1 = lax.ppermute(halo_1, "context", TO_CORE_1)
    added, x_conv, bc_conv, cum, delta = call(
        conv_kernel,
        (
            shaped((HEADS, P_SIZE + 16, N), BF16),
            shaped((CHIP, HALF), BF16),
            shaped((CHIP, 512), BF16),
            shaped((CHIP, 128), F32),
            shaped((CHIP, 128), F32),
        ),
        scratch=[
            pltpu.VMEM((CHIP + 16, 1024), F32),
            pltpu.VMEM((CHIP, 128), F32),
            pltpu.VMEM((CHIP, HALF), BF16),
            pltpu.VMEM((CHIP, 512), BF16),
            pltpu.VMEM((CHIP, 128), F32),
            pltpu.VMEM((CHIP, 128), F32),
            pltpu.VMEM((ROWS, HALF), BF16),
            pltpu.VMEM((ROWS, 640), BF16),
            pltpu.VMEM((ROWS, 1152), BF16),
            pltpu.VMEM((16, 1024), BF16),
            pltpu.VMEM((16, 1024), BF16),
            pltpu.VMEM((32, 1024), F32),
            pltpu.SemaphoreType.DMA((10,)),
        ],
        in_specs=[HBM] * 6,
        out_specs=[VMEM] + [HBM] * 4,
        limit=WIDE,
        flops=200_000_000,
        moved=2 << 20,
    )(mine, sent, got, halo_0, halo_1, fixed)
    increments = lax.all_to_all(added, "context", 0, 0, tiled=True, axis_index_groups=SAME_CORE)
    inside = call(
        inside_kernel,
        shaped((CHIP, HALF), F32),
        scratch=[
            pltpu.VMEM((CHIP, HALF), BF16),
            pltpu.VMEM((CHIP, 512), BF16),
            pltpu.VMEM((CHIP, 128), F32),
            pltpu.VMEM((CHIP, 128), F32),
            pltpu.VMEM((CHIP, HALF), F32),
            pltpu.SemaphoreType.DMA((4,)),
        ],
        in_specs=[HBM] * 4 + [SMEM],
        out_specs=HBM,
        flops=400_000_000,
        moved=2 << 20,
    )(x_conv, bc_conv, cum, delta, d_skip)
    increments, inside = lax.optimization_barrier((increments, inside))
    first = lax.dynamic_index_in_dim(init_state, core * HEADS + chip, 0, keepdims=False)
    states = call(
        prefix_kernel,
        shaped((CHIPS, P_SIZE, N), BF16),
        in_specs=[VMEM] * 2,
        moved=1 << 20,
    )(increments, first)
    states = lax.all_to_all(states, "context", 0, 0, tiled=True, axis_index_groups=SAME_CORE)
    states, weights = lax.optimization_barrier((states, weights))
    weights = lax.all_gather(weights, "context", axis=0, tiled=True, axis_index_groups=CORES)
    weights = weights.reshape(4, 1024, HALF)
    gain = norm_gain.reshape(1, 1024)
    keep, to_core, to_next, to_cross = call(
        carry_kernel,
        (shaped((80, HALF), BF16),) * 4,
        scratch=[
            pltpu.VMEM((HEADS * P_SIZE, N), BF16),
            pltpu.VMEM((CHIP, N), BF16),
            pltpu.VMEM((CHIP, 128), F32),
            pltpu.VMEM((CHIP, HALF), F32),
            pltpu.VMEM((CHIP, HALF), BF16),
            pltpu.VMEM((1, 1024), F32),
            pltpu.VMEM((2, 4, 2, 16, HALF), BF16),
            pltpu.SemaphoreType.DMA((7,)),
        ],
        in_specs=[HBM] * 7,
        out_specs=[VMEM] * 4,
        limit=WIDE,
        flops=100_000_000,
        moved=2 << 20,
    )(states.reshape(HEADS * P_SIZE, N), bc_conv, cum, inside, zs, got, gain)
    core_got = lax.ppermute(to_core, "context", PAIR)
    next_got = lax.ppermute(to_next, "tensor", BESIDE)
    cross_got = lax.ppermute(to_cross, ("context", "tensor"), CROSS)
    normed = call(
        norm_kernel,
        shaped((64, 2048), BF16),
        in_specs=[VMEM] * 4,
        out_specs=VMEM,
        moved=1 << 20,
    )(keep, core_got, next_got, cross_got)

    up, down = [normed], [normed]
    for step in range(4):
        up.append(lax.ppermute(up[-1], "context", UP))
        if step < 3:
            down.append(lax.ppermute(down[-1], "context", DOWN))
    blocks = {**{r: up[r] for r in range(5)}, **{CHIPS - r: down[r] for r in range(1, 4)}}
    near = product([blocks[r] for r in NEAR], weights)
    far = product([blocks[r] for r in FAR], weights)
    near = lax.psum_scatter(
        near.reshape(4 * 16 * len(NEAR), 1024), "tensor",
        scatter_dimension=0, tiled=True, axis_index_groups=PARITY,
    )
    far = lax.all_to_all(
        far.reshape(4, 16 * len(FAR), 1024), "tensor", 0, 0, tiled=True, axis_index_groups=PARITY
    )
    ready = call(
        collect_kernel,
        shaped((CHIPS, 16, 1024), BF16),
        scratch=[pltpu.VMEM((len(NEAR), 16, 1024), BF16), pltpu.SemaphoreType.DMA((1,))],
        in_specs=[HBM, VMEM],
        moved=2 << 20,
    )(near.reshape(len(NEAR), 16, 1024), far.reshape(4, len(FAR), 16, 1024))
    return lax.all_to_all(
        ready, "context", 0, 0, tiled=True, axis_index_groups=SAME_CORE
    ).transpose(1, 0, 2).reshape(16, 8192)


def solution(mesh):
    return jax.shard_map(
        body,
        mesh=mesh,
        in_specs=(
            P(("dp", "context"), "tensor"),
            P(("dp", "context"), None, "tensor"),
            P(("dp", "context"), "tensor"),
            P(("dp", "context"), "tensor"),
            P("dp", "tensor"),
            P("dp", None, "tensor"),
            P(None, "tensor"),
            P(None, None, "tensor"),
            P("tensor"),
            P("tensor"),
            P("tensor"),
            P(("dp", "tensor"), None, None),
            P("tensor"),
            P("tensor", "context"),
        ),
        out_specs=P(("dp", "context", "tensor"), None),
        check_vma=False,
    )
```

```python
import functools

import jax
import jax.numpy as jnp
from jax import lax
from jax.experimental import pallas as pl
from jax.experimental.pallas import tpu as pltpu
from jax.sharding import PartitionSpec as P

ROWS = 128
CHIP = 256
HALF = 512
HEADS = 8
P_SIZE = 64
N = 256
CHIPS = 8
PAIR = [(i, i ^ 1) for i in range(16)]
SAME_CORE = [[2 * i + k for i in range(CHIPS)] for k in range(2)]
UP = [(i, (i + 2) % 16) for i in range(16)]
DOWN = [(i, (i - 2) % 16) for i in range(16)]
CROSS = [(8 * i + t, 8 * (i ^ 1) + (t ^ 1)) for i in range(16) for t in range(8)]
BESIDE = [(t, t ^ 1) for t in range(8)]
PARITY = [[0, 2, 4, 6], [1, 3, 5, 7]]
CORES = [[2 * i, 2 * i + 1] for i in range(CHIPS)]
BOTH = [[0, 1], [2, 3], [4, 5], [6, 7]]
NEAR = (0, 1, 7, 2, 6)
FAR = (3, 5, 4)
TO_CORE_0 = [(2 * i + 1, 2 * i + 2) for i in range(CHIPS - 1)]
TO_CORE_1 = [(2 * i + 1, 2 * i + 3) for i in range(CHIPS - 1)]
F32 = jnp.float32
BF16 = jnp.bfloat16
EXACT = lax.Precision.HIGHEST
LIMIT = 24 * 1024 * 1024
WIDE = 63 * 1024 * 1024


def call(kernel, out_shape, scratch=(), flops=0, moved=0, limit=LIMIT, **kwargs):
    return pl.pallas_call(
        kernel,
        out_shape=out_shape,
        scratch_shapes=list(scratch),
        compiler_params=pltpu.CompilerParams(vmem_limit_bytes=limit),
        cost_estimate=pl.CostEstimate(flops=flops, bytes_accessed=moved, transcendentals=0),
        **kwargs,
    )


VMEM = pl.BlockSpec(memory_space=pltpu.VMEM)
HBM = pl.BlockSpec(memory_space=pltpu.HBM)


def shaped(shape, dtype):
    return jax.ShapeDtypeStruct(shape, dtype)


def silu(v):
    return v / (1.0 + jnp.exp(-v))


def half_of(ref, core):
    return ref[:, pl.ds(pl.multiple_of(core * HALF, HALF), HALF)]


def spread():
    head = lax.broadcasted_iota(jnp.int32, (128, HALF), 0)
    lane = lax.broadcasted_iota(jnp.int32, (128, HALF), 1)
    return (lane // P_SIZE == head).astype(F32)


def place():
    position = lax.axis_index("context")
    return lax.rem(position, 2), lax.div(position, 2)


def copies(pairs, sems):
    return [pltpu.make_async_copy(source, target, sems.at[i]) for i, (source, target) in enumerate(pairs)]


def fetch(pairs, sems):
    moving = copies(pairs, sems)
    for copy in moving:
        copy.start()
    for copy in moving:
        copy.wait()


def lanes(core):
    return pl.ds(pl.multiple_of(core * HALF, HALF), HALF)


def tokens(core):
    return pl.ds(pl.multiple_of(core * ROWS, ROWS), ROWS)


TAPS, BIAS, RATE = 16, 20, 21


def pack_kernel(
    xs, zs, bcs, dt, tail_x, tail_bc, taps_x, taps_bc, bias, rate,
    send, halo_0, halo_1, mine, fixed, b_c, steps, tail_2, tail_3, taps_2, taps_3, bias_1, rate_1, heads, sems,
):
    core, _ = place()
    heads[...] = jnp.zeros((2, 128), F32)
    fetch(
        [
            (bcs, b_c),
            (dt, steps),
            (tail_x, tail_2),
            (tail_bc, tail_3),
            (taps_x, taps_2),
            (taps_bc, taps_3),
            (bias, bias_1),
            (rate, rate_1),
            (xs.at[:, lanes(1 - core)], send.at[:, 0:512]),
            (zs.at[:, lanes(1 - core)], send.at[:, 1152:1664]),
            (xs.at[:, lanes(core)], mine),
            (xs.at[112:128, 0:512], halo_0.at[:, 0:512]),
            (xs.at[112:128, 512:1024], halo_1.at[:, 0:512]),
        ],
        sems,
    )
    send[:, 512:768] = b_c[:, 0, :]
    send[:, 768:1024] = b_c[:, 1, :]
    by_head = jnp.concatenate([steps[...].astype(F32), jnp.zeros((112, ROWS), F32)], axis=0)
    send[:, 1024:1152] = jnp.transpose(by_head).astype(BF16)
    halo_0[:, 512:1024] = send[112:128, 512:1024]
    halo_1[:, 512:1024] = send[112:128, 512:1024]
    fixed[...] = jnp.zeros((32, 1024), F32)
    fixed[13:16, 0:512] = half_of(tail_2, core).astype(F32)
    fixed[13:16, 512:768] = tail_3[:, 0, :].astype(F32)
    fixed[13:16, 768:1024] = tail_3[:, 1, :].astype(F32)
    fixed[TAPS : TAPS + 4, 0:512] = half_of(taps_2, core).astype(F32)
    fixed[TAPS : TAPS + 4, 512:768] = taps_3[:, 0, :].astype(F32)
    fixed[TAPS : TAPS + 4, 768:1024] = taps_3[:, 1, :].astype(F32)
    heads[0:1, 0:16] = bias_1[...]
    heads[1:2, 0:16] = rate_1[...]
    own = jnp.where(core == 0, heads[...], pltpu.roll(heads[...], 120, 1))
    fixed[BIAS : BIAS + 1, 0:128] = own[0:1]
    fixed[RATE : RATE + 1, 0:128] = -jnp.exp(own[1:2])


def conv_kernel(
    xs_in, sent_in, got_in, halo_0_in, halo_1_in, fixed_in,
    added_out, x_out, bc_out, cum_out, delta_out, rows, steps, x_conv, bc_conv, cums, deltas,
    xs, sent, got, halo_0, halo_1, fixed, sems,
):
    core, chip = place()
    mine, other = tokens(core), tokens(1 - core)
    fetch(
        [
            (xs_in, xs),
            (sent_in.at[:, 512:1152], sent),
            (got_in.at[:, 0:1152], got),
            (halo_0_in, halo_0),
            (halo_1_in, halo_1),
            (fixed_in, fixed),
        ],
        sems.at[4:10],
    )
    first = pl.multiple_of(core * ROWS + 16, 16)
    second = pl.multiple_of((1 - core) * ROWS + 16, 16)
    rows[pl.ds(first, ROWS), 0:512] = xs[...].astype(F32)
    rows[pl.ds(first, ROWS), 512:1024] = sent[:, 0:512].astype(F32)
    rows[pl.ds(second, ROWS), :] = got[:, 0:1024].astype(F32)
    halo = halo_0[...].astype(F32) + halo_1[...].astype(F32)
    rows[0:16, :] = jnp.where(chip == 0, fixed[0:16, :], halo)
    for lane in range(0, 1024, 128):
        cut = slice(lane, lane + 128)
        total = fixed[TAPS : TAPS + 1, cut] * rows[13 : 13 + CHIP, cut]
        for k in range(1, 4):
            total = total + fixed[TAPS + k : TAPS + k + 1, cut] * rows[13 + k : 13 + k + CHIP, cut]
        value = silu(total).astype(BF16)
        if lane < 512:
            x_conv[:, cut] = value
        else:
            bc_conv[:, lane - 512 : lane - 384] = value
    steps[mine, :] = sent[:, 512:640].astype(F32)
    steps[other, :] = got[:, 1024:1152].astype(F32)
    raw = jnp.where(core == 0, steps[...], pltpu.roll(steps[...], 120, 1)) + fixed[BIAS : BIAS + 1, 0:128]
    delta = jnp.maximum(raw, 0.0) + jnp.log(1.0 + jnp.exp(-jnp.abs(raw)))
    logs = delta * fixed[RATE : RATE + 1, 0:128]
    row = lax.broadcasted_iota(jnp.int32, (CHIP, CHIP), 0)
    column = lax.broadcasted_iota(jnp.int32, (CHIP, CHIP), 1)
    cum = jnp.dot((row >= column).astype(F32), logs, precision=EXACT, preferred_element_type=F32)
    cums[...] = cum
    deltas[...] = delta
    kept = copies(
        [(x_conv, x_out), (bc_conv, bc_out), (cums, cum_out), (deltas, delta_out)],
        sems.at[0:4],
    )
    for copy in kept:
        copy.start()
    last = cum[CHIP - 1 : CHIP, :]
    trailing = jnp.dot(jnp.exp(last - cum) * delta, spread(), precision=EXACT, preferred_element_type=F32)
    weighted = (x_conv[...].astype(F32) * trailing).astype(BF16)
    added = lax.dot_general(
        weighted, bc_conv[:, 0:N], (((0,), (0,)), ((), ())), preferred_element_type=F32
    )
    high = last.astype(BF16).astype(F32)
    middle = (last - high).astype(BF16).astype(F32)
    low = last - high - middle
    line = lax.broadcasted_iota(jnp.int32, (16, N), 0)
    for h in range(HEADS):
        added_out[h, 0:P_SIZE, :] = added[h * P_SIZE : (h + 1) * P_SIZE].astype(BF16)
        terms = jnp.where(
            line == 0,
            jnp.broadcast_to(high[:, h : h + 1], (16, N)),
            jnp.where(
                line == 1,
                jnp.broadcast_to(middle[:, h : h + 1], (16, N)),
                jnp.where(line == 2, jnp.broadcast_to(low[:, h : h + 1], (16, N)), 0.0),
            ),
        )
        added_out[h, P_SIZE : P_SIZE + 16, :] = terms.astype(BF16)
    for copy in kept:
        copy.wait()


def inside_kernel(x_in, bc_in, cum_in, delta_in, skip_in, out, x, bc, cum, delta, skip, total, sems):
    core, _ = place()
    fetch([(x_in, x), (bc_in, bc), (cum_in, cum), (delta_in, delta), (skip_in, skip)], sems)
    scores = lax.dot_general(
        bc[:, N : 2 * N], bc[:, 0:N], (((1,), (1,)), ((), ())), preferred_element_type=F32
    )
    row = lax.broadcasted_iota(jnp.int32, (CHIP, CHIP), 0)
    column = lax.broadcasted_iota(jnp.int32, (CHIP, CHIP), 1)
    scores = jnp.where(row >= column, scores, 0.0)
    cum_t = jnp.transpose(cum[...])
    delta_t = jnp.transpose(delta[...])
    lane = lax.broadcasted_iota(jnp.int32, (CHIP, 128), 1)
    for pair in range(HEADS // 2):
        cut = slice(pair * 128, pair * 128 + 128)
        values = x[:, cut]
        both = []
        for h in (2 * pair, 2 * pair + 1):
            decay = jnp.exp(jnp.minimum(cum[:, h : h + 1] - cum_t[h : h + 1, :], 0.0))
            weights = (decay * scores * delta_t[h : h + 1, :]).astype(BF16)
            scale = jnp.where(core == 0, skip[:, h : h + 1], skip[:, HEADS + h : HEADS + h + 1])
            through = scale * values.astype(F32)
            both.append(jnp.dot(weights, values, preferred_element_type=F32) + through)
        total[:, cut] = jnp.where(lane < P_SIZE, both[0], both[1])
    fetch([(total, out)], sems)


def prefix_kernel(got, first, out):
    state = first[...]
    for chip in range(CHIPS):
        out[chip] = state.astype(BF16)
        if chip < CHIPS - 1:
            terms = got[chip, P_SIZE : P_SIZE + 16, :].astype(F32)
            decay = jnp.exp(terms[0:1] + terms[1:2] + terms[2:3])
            state = decay * state + got[chip, 0:P_SIZE, :].astype(F32)


def carry_kernel(
    state_in, bc_in, cum_in, inside_in, zs, got, gain_in,
    keep, to_core, to_next, to_cross, state, c, cum, inside, gate, gain, pieces, sems,
):
    core, _ = place()
    fetch(
        [
            (bc_in.at[:, N : 2 * N], c),
            (cum_in, cum),
            (inside_in, inside),
            (zs.at[:, lanes(core)], gate.at[tokens(core), :]),
            (got.at[:, 1152:1664], gate.at[tokens(1 - core), :]),
            (state_in, state),
            (gain_in, gain),
        ],
        sems,
    )
    carried = lax.dot_general(
        c[...], state[...], (((1,), (1,)), ((), ())), preferred_element_type=F32
    )
    decay = jnp.dot(jnp.exp(cum[...]), spread(), precision=EXACT, preferred_element_type=F32)
    gated = (inside[...] + carried * decay) * silu(gate[...].astype(F32))
    pieces[...] = gated.astype(BF16).reshape(2, 4, 2, 16, HALF)

    def piece(side, parity):
        return pieces[pl.ds(side, 1), :, pl.ds(parity, 1)].reshape(64, HALF)

    odd = lax.rem(lax.axis_index("tensor"), 2)
    whole = gain[:, lanes(core)]
    high = whole.astype(BF16).astype(F32)
    middle = (whole - high).astype(BF16).astype(F32)
    low = whole - high - middle
    line = lax.broadcasted_iota(jnp.int32, (16, HALF), 0)
    terms = jnp.where(line == 0, high, jnp.where(line == 1, middle, jnp.where(line == 2, low, 0.0)))
    for out, side, parity in (
        (keep, core, odd), (to_core, 1 - core, odd), (to_next, core, 1 - odd), (to_cross, 1 - core, 1 - odd),
    ):
        out[0:64, :] = piece(side, parity)
        out[64:80, :] = terms.astype(BF16)


def norm_kernel(keep, core_got, next_got, cross_got, out):
    core, _ = place()
    odd = lax.rem(lax.axis_index("tensor"), 2)
    for mine, came, position in ((keep, core_got, odd), (next_got, cross_got, 1 - odd)):
        values = [ref[0:64, :].astype(F32) for ref in (mine, came)]
        squares = jnp.sum(values[0] * values[0] + values[1] * values[1], axis=1, keepdims=True)
        factor = lax.rsqrt(squares * (1.0 / 1024.0) + 1e-05)
        for ref, value, side in ((mine, values[0], core), (came, values[1], 1 - core)):
            terms = ref[64:80, :].astype(F32)
            gain = terms[0:1] + terms[1:2] + terms[2:3]
            at = pl.ds(pl.multiple_of(position * 1024 + side * HALF, HALF), HALF)
            out[:, at] = (value * factor * gain).astype(BF16)


def stage_kernel(source, out, sems):
    fetch([(source.at[i], out.at[i]) for i in range(4)], sems)


def product_kernel(*refs):
    *blocks, weights, out, rows, result, sems = refs
    count = len(blocks)
    for r, block in enumerate(blocks):
        rows[r * 64 : (r + 1) * 64, :] = block[...]
    moving = []
    for side in range(2):
        value = jnp.dot(rows[:, 0:1024], weights[2 * side], preferred_element_type=F32)
        value = value + jnp.dot(rows[:, 1024:2048], weights[2 * side + 1], preferred_element_type=F32)
        value = value.astype(BF16)
        for r in range(count):
            result[side, :, r] = value[r * 64 : (r + 1) * 64].reshape(4, 16, HALF)
        copy = pltpu.make_async_copy(
            result.at[side], out.at[:, :, :, side * HALF : (side + 1) * HALF], sems.at[side]
        )
        copy.start()
        moving.append(copy)
    for copy in moving:
        copy.wait()


def product(blocks, weights):
    count = len(blocks)
    return call(
        product_kernel,
        shaped((4, count, 16, 1024), BF16),
        scratch=[
            pltpu.VMEM((count * 64, 2048), BF16),
            pltpu.VMEM((2, 4, count, 16, HALF), BF16),
            pltpu.SemaphoreType.DMA((2,)),
        ],
        in_specs=[VMEM] * (count + 1),
        out_specs=HBM,
        flops=count * 270_000_000,
        moved=6 << 20,
    )(*blocks, weights)


def summed_over(terms, unit):
    total = terms[0, unit].astype(F32)
    for source in range(1, 4):
        total = total + terms[source, unit].astype(F32)
    return total.astype(BF16)


def collect_kernel(near, far, out, summed, sems):
    _, chip = place()
    moving = copies([(near, summed)], sems)
    moving[0].start()
    for r, before in enumerate(FAR):
        out[lax.rem(chip + (CHIPS - before), CHIPS)] = summed_over(far, r)
    moving[0].wait()
    for r, before in enumerate(NEAR):
        out[lax.rem(chip + (CHIPS - before), CHIPS)] = summed[r]


def body(
    xs, bcs, zs, dt_raw, tail_x, tail_bc, conv_x, conv_bc,
    dt_bias, a_log, d_skip, init_state, norm_gain, out_weight,
):
    core, chip = place()
    weights = lax.all_gather(out_weight, "tensor", axis=0, tiled=True, axis_index_groups=BOTH)
    sent, halo_0, halo_1, mine, fixed = call(
        pack_kernel,
        (
            shaped((ROWS, 1664), BF16),
            shaped((16, 1024), BF16),
            shaped((16, 1024), BF16),
            shaped((ROWS, HALF), BF16),
            shaped((32, 1024), F32),
        ),
        scratch=[
            pltpu.VMEM((ROWS, 2, N), BF16),
            pltpu.VMEM((16, ROWS), BF16),
            pltpu.VMEM((3, 1024), BF16),
            pltpu.VMEM((3, 2, N), BF16),
            pltpu.VMEM((4, 1024), BF16),
            pltpu.VMEM((4, 2, N), BF16),
            pltpu.VMEM((1, 16), F32),
            pltpu.VMEM((1, 16), F32),
            pltpu.VMEM((2, 128), F32),
            pltpu.SemaphoreType.DMA((13,)),
        ],
        in_specs=[HBM] * 10,
        out_specs=[VMEM] * 5,
        moved=1 << 20,
        limit=WIDE,
    )(
        xs, zs, bcs, dt_raw.T, tail_x, tail_bc, conv_x, conv_bc,
        dt_bias.reshape(1, 16), a_log.reshape(1, 16),
    )
    got = lax.ppermute(sent, "context", PAIR)
    halo_0 = lax.ppermute(halo_0, "context", TO_CORE_0)
    halo_1 = lax.ppermute(halo_1, "context", TO_CORE_1)
    added, x_conv, bc_conv, cum, delta = call(
        conv_kernel,
        (
            shaped((HEADS, P_SIZE + 16, N), BF16),
            shaped((CHIP, HALF), BF16),
            shaped((CHIP, 512), BF16),
            shaped((CHIP, 128), F32),
            shaped((CHIP, 128), F32),
        ),
        scratch=[
            pltpu.VMEM((CHIP + 16, 1024), F32),
            pltpu.VMEM((CHIP, 128), F32),
            pltpu.VMEM((CHIP, HALF), BF16),
            pltpu.VMEM((CHIP, 512), BF16),
            pltpu.VMEM((CHIP, 128), F32),
            pltpu.VMEM((CHIP, 128), F32),
            pltpu.VMEM((ROWS, HALF), BF16),
            pltpu.VMEM((ROWS, 640), BF16),
            pltpu.VMEM((ROWS, 1152), BF16),
            pltpu.VMEM((16, 1024), BF16),
            pltpu.VMEM((16, 1024), BF16),
            pltpu.VMEM((32, 1024), F32),
            pltpu.SemaphoreType.DMA((10,)),
        ],
        in_specs=[HBM] * 6,
        out_specs=[VMEM] + [HBM] * 4,
        limit=WIDE,
        flops=200_000_000,
        moved=2 << 20,
    )(mine, sent, got, halo_0, halo_1, fixed)
    increments = lax.all_to_all(added, "context", 0, 0, tiled=True, axis_index_groups=SAME_CORE)
    inside = call(
        inside_kernel,
        shaped((CHIP, HALF), F32),
        scratch=[
            pltpu.VMEM((CHIP, HALF), BF16),
            pltpu.VMEM((CHIP, 512), BF16),
            pltpu.VMEM((CHIP, 128), F32),
            pltpu.VMEM((CHIP, 128), F32),
            pltpu.VMEM((1, 16), F32),
            pltpu.VMEM((CHIP, HALF), F32),
            pltpu.SemaphoreType.DMA((5,)),
        ],
        in_specs=[HBM] * 5,
        out_specs=HBM,
        flops=400_000_000,
        moved=2 << 20,
        limit=WIDE,
    )(x_conv, bc_conv, cum, delta, d_skip.reshape(1, 16))
    increments, inside = lax.optimization_barrier((increments, inside))
    first = lax.dynamic_index_in_dim(init_state, core * HEADS + chip, 0, keepdims=False)
    states = call(
        prefix_kernel,
        shaped((CHIPS, P_SIZE, N), BF16),
        in_specs=[VMEM] * 2,
        moved=1 << 20,
    )(increments, first)
    states = lax.all_to_all(states, "context", 0, 0, tiled=True, axis_index_groups=SAME_CORE)
    states, weights = lax.optimization_barrier((states, weights))
    weights = lax.all_gather(weights, "context", axis=0, tiled=True, axis_index_groups=CORES)
    weights = weights.reshape(4, 1024, HALF)
    gain = norm_gain.reshape(1, 1024)
    keep, to_core, to_next, to_cross = call(
        carry_kernel,
        (shaped((80, HALF), BF16),) * 4,
        scratch=[
            pltpu.VMEM((HEADS * P_SIZE, N), BF16),
            pltpu.VMEM((CHIP, N), BF16),
            pltpu.VMEM((CHIP, 128), F32),
            pltpu.VMEM((CHIP, HALF), F32),
            pltpu.VMEM((CHIP, HALF), BF16),
            pltpu.VMEM((1, 1024), F32),
            pltpu.VMEM((2, 4, 2, 16, HALF), BF16),
            pltpu.SemaphoreType.DMA((7,)),
        ],
        in_specs=[HBM] * 7,
        out_specs=[VMEM] * 4,
        limit=WIDE,
        flops=100_000_000,
        moved=2 << 20,
    )(states.reshape(HEADS * P_SIZE, N), bc_conv, cum, inside, zs, got, gain)
    cross_got = lax.ppermute(to_cross, ("context", "tensor"), CROSS)
    next_got = lax.ppermute(to_next, "tensor", BESIDE)
    core_got = lax.ppermute(to_core, "context", PAIR)
    normed = call(
        norm_kernel,
        shaped((64, 2048), BF16),
        in_specs=[VMEM] * 4,
        out_specs=VMEM,
        moved=1 << 20,
    )(keep, core_got, next_got, cross_got)

    def staged(weights):
        return call(
            stage_kernel,
            shaped((4, 1024, HALF), BF16),
            scratch=[pltpu.SemaphoreType.DMA((4,))],
            in_specs=[HBM],
            out_specs=VMEM,
            moved=8 << 20,
            limit=48 * 1024 * 1024,
        )(weights)

    up, down = [normed], [normed]
    for step in range(4):
        if step == 1:
            up[1], weights = lax.optimization_barrier((up[1], weights))
        up.append(lax.ppermute(up[-1], "context", UP))
        if step < 3:
            down.append(lax.ppermute(down[-1], "context", DOWN))
    blocks = {**{r: up[r] for r in range(5)}, **{CHIPS - r: down[r] for r in range(1, 4)}}
    near = product([blocks[r] for r in NEAR], staged(weights))
    blocks[3], weights = lax.optimization_barrier((blocks[3], weights))
    far = product([blocks[r] for r in FAR], staged(weights))
    near = lax.psum_scatter(
        near.reshape(4 * 16 * len(NEAR), 1024), "tensor",
        scatter_dimension=0, tiled=True, axis_index_groups=PARITY,
    )
    far = lax.all_to_all(
        far.reshape(4, 16 * len(FAR), 1024), "tensor", 0, 0, tiled=True, axis_index_groups=PARITY
    )
    ready = call(
        collect_kernel,
        shaped((CHIPS, 16, 1024), BF16),
        scratch=[pltpu.VMEM((len(NEAR), 16, 1024), BF16), pltpu.SemaphoreType.DMA((1,))],
        in_specs=[HBM, VMEM],
        moved=2 << 20,
    )(near.reshape(len(NEAR), 16, 1024), far.reshape(4, len(FAR), 16, 1024))
    return lax.all_to_all(
        ready, "context", 0, 0, tiled=True, axis_index_groups=SAME_CORE
    ).transpose(1, 0, 2).reshape(16, 8192)


def solution(mesh):
    return jax.shard_map(
        body,
        mesh=mesh,
        in_specs=(
            P(("dp", "context"), "tensor"),
            P(("dp", "context"), None, "tensor"),
            P(("dp", "context"), "tensor"),
            P(("dp", "context"), "tensor"),
            P("dp", "tensor"),
            P("dp", None, "tensor"),
            P(None, "tensor"),
            P(None, None, "tensor"),
            P("tensor"),
            P("tensor"),
            P("tensor"),
            P(("dp", "tensor"), None, None),
            P("tensor"),
            P("tensor", "context"),
        ),
        out_specs=P(("dp", "context", "tensor"), None),
        check_vma=False,
    )
```

```python
import functools

import jax
import jax.numpy as jnp
from jax import lax
from jax.experimental import pallas as pl
from jax.experimental.pallas import tpu as pltpu
from jax.sharding import PartitionSpec as P

ROWS = 128
CHIP = 256
HALF = 512
HEADS = 8
P_SIZE = 64
N = 256
CHIPS = 8
PAIR = [(i, i ^ 1) for i in range(16)]
SAME_CORE = [[2 * i + k for i in range(CHIPS)] for k in range(2)]
UP = [(i, (i + 2) % 16) for i in range(16)]
DOWN = [(i, (i - 2) % 16) for i in range(16)]
CROSS = [(8 * i + t, 8 * (i ^ 1) + (t ^ 1)) for i in range(16) for t in range(8)]
BESIDE = [(t, t ^ 1) for t in range(8)]
PARITY = [[0, 2, 4, 6], [1, 3, 5, 7]]
CORES = [[2 * i, 2 * i + 1] for i in range(CHIPS)]
BOTH = [[0, 1], [2, 3], [4, 5], [6, 7]]
NEAR = (0, 1, 7, 2, 6)
FAR = (3, 5, 4)
TO_CORE_0 = [(2 * i + 1, 2 * i + 2) for i in range(CHIPS - 1)]
TO_CORE_1 = [(2 * i + 1, 2 * i + 3) for i in range(CHIPS - 1)]
F32 = jnp.float32
BF16 = jnp.bfloat16
EXACT = lax.Precision.HIGHEST
LIMIT = 24 * 1024 * 1024
WIDE = 63 * 1024 * 1024


def call(kernel, out_shape, scratch=(), flops=0, moved=0, limit=LIMIT, **kwargs):
    return pl.pallas_call(
        kernel,
        out_shape=out_shape,
        scratch_shapes=list(scratch),
        compiler_params=pltpu.CompilerParams(vmem_limit_bytes=limit),
        cost_estimate=pl.CostEstimate(flops=flops, bytes_accessed=moved, transcendentals=0),
        **kwargs,
    )


VMEM = pl.BlockSpec(memory_space=pltpu.VMEM)
HBM = pl.BlockSpec(memory_space=pltpu.HBM)


def shaped(shape, dtype):
    return jax.ShapeDtypeStruct(shape, dtype)


def silu(v):
    return v / (1.0 + jnp.exp(-v))


def half_of(ref, core):
    return ref[:, pl.ds(pl.multiple_of(core * HALF, HALF), HALF)]


def spread():
    head = lax.broadcasted_iota(jnp.int32, (128, HALF), 0)
    lane = lax.broadcasted_iota(jnp.int32, (128, HALF), 1)
    return (lane // P_SIZE == head).astype(F32)


def place():
    position = lax.axis_index("context")
    return lax.rem(position, 2), lax.div(position, 2)


def copies(pairs, sems):
    return [pltpu.make_async_copy(source, target, sems.at[i]) for i, (source, target) in enumerate(pairs)]


def fetch(pairs, sems):
    moving = copies(pairs, sems)
    for copy in moving:
        copy.start()
    for copy in moving:
        copy.wait()


def lanes(core):
    return pl.ds(pl.multiple_of(core * HALF, HALF), HALF)


def tokens(core):
    return pl.ds(pl.multiple_of(core * ROWS, ROWS), ROWS)


TAPS, BIAS, RATE = 16, 20, 21


def pack_kernel(
    xs, zs, bcs, dt, tail_x, tail_bc, taps_x, taps_bc, bias, rate,
    send, halo_0, halo_1, mine, fixed, b_c, steps, tail_2, tail_3, taps_2, taps_3, bias_1, rate_1, heads, sems,
):
    core, _ = place()
    heads[...] = jnp.zeros((2, 128), F32)
    fetch(
        [
            (bcs, b_c),
            (dt, steps),
            (tail_x, tail_2),
            (tail_bc, tail_3),
            (taps_x, taps_2),
            (taps_bc, taps_3),
            (bias, bias_1),
            (rate, rate_1),
            (xs.at[:, lanes(1 - core)], send.at[:, 0:512]),
            (zs.at[:, lanes(1 - core)], send.at[:, 1152:1664]),
            (xs.at[:, lanes(core)], mine),
            (xs.at[112:128, 0:512], halo_0.at[:, 0:512]),
            (xs.at[112:128, 512:1024], halo_1.at[:, 0:512]),
        ],
        sems,
    )
    send[:, 512:768] = b_c[:, 0, :]
    send[:, 768:1024] = b_c[:, 1, :]
    by_head = jnp.concatenate([steps[...].astype(F32), jnp.zeros((112, ROWS), F32)], axis=0)
    send[:, 1024:1152] = jnp.transpose(by_head).astype(BF16)
    halo_0[:, 512:1024] = send[112:128, 512:1024]
    halo_1[:, 512:1024] = send[112:128, 512:1024]
    fixed[...] = jnp.zeros((32, 1024), F32)
    fixed[13:16, 0:512] = half_of(tail_2, core).astype(F32)
    fixed[13:16, 512:768] = tail_3[:, 0, :].astype(F32)
    fixed[13:16, 768:1024] = tail_3[:, 1, :].astype(F32)
    fixed[TAPS : TAPS + 4, 0:512] = half_of(taps_2, core).astype(F32)
    fixed[TAPS : TAPS + 4, 512:768] = taps_3[:, 0, :].astype(F32)
    fixed[TAPS : TAPS + 4, 768:1024] = taps_3[:, 1, :].astype(F32)
    heads[0:1, 0:16] = bias_1[...]
    heads[1:2, 0:16] = rate_1[...]
    own = jnp.where(core == 0, heads[...], pltpu.roll(heads[...], 120, 1))
    fixed[BIAS : BIAS + 1, 0:128] = own[0:1]
    fixed[RATE : RATE + 1, 0:128] = -jnp.exp(own[1:2])


def conv_kernel(
    xs_in, sent_in, got_in, halo_0_in, halo_1_in, fixed_in,
    added_out, x_out, bc_out, cum_out, delta_out, rows, steps, x_conv, bc_conv, cums, deltas,
    xs, sent, got, halo_0, halo_1, fixed, sems,
):
    core, chip = place()
    mine, other = tokens(core), tokens(1 - core)
    fetch(
        [
            (xs_in, xs),
            (sent_in.at[:, 512:1152], sent),
            (got_in.at[:, 0:1152], got),
            (halo_0_in, halo_0),
            (halo_1_in, halo_1),
            (fixed_in, fixed),
        ],
        sems.at[4:10],
    )
    first = pl.multiple_of(core * ROWS + 16, 16)
    second = pl.multiple_of((1 - core) * ROWS + 16, 16)
    rows[pl.ds(first, ROWS), 0:512] = xs[...].astype(F32)
    rows[pl.ds(first, ROWS), 512:1024] = sent[:, 0:512].astype(F32)
    rows[pl.ds(second, ROWS), :] = got[:, 0:1024].astype(F32)
    halo = halo_0[...].astype(F32) + halo_1[...].astype(F32)
    rows[0:16, :] = jnp.where(chip == 0, fixed[0:16, :], halo)
    for lane in range(0, 1024, 128):
        cut = slice(lane, lane + 128)
        total = fixed[TAPS : TAPS + 1, cut] * rows[13 : 13 + CHIP, cut]
        for k in range(1, 4):
            total = total + fixed[TAPS + k : TAPS + k + 1, cut] * rows[13 + k : 13 + k + CHIP, cut]
        value = silu(total).astype(BF16)
        if lane < 512:
            x_conv[:, cut] = value
        else:
            bc_conv[:, lane - 512 : lane - 384] = value
    steps[mine, :] = sent[:, 512:640].astype(F32)
    steps[other, :] = got[:, 1024:1152].astype(F32)
    raw = jnp.where(core == 0, steps[...], pltpu.roll(steps[...], 120, 1)) + fixed[BIAS : BIAS + 1, 0:128]
    delta = jnp.maximum(raw, 0.0) + jnp.log(1.0 + jnp.exp(-jnp.abs(raw)))
    logs = delta * fixed[RATE : RATE + 1, 0:128]
    row = lax.broadcasted_iota(jnp.int32, (CHIP, CHIP), 0)
    column = lax.broadcasted_iota(jnp.int32, (CHIP, CHIP), 1)
    cum = jnp.dot((row >= column).astype(F32), logs, precision=EXACT, preferred_element_type=F32)
    cums[...] = cum
    deltas[...] = delta
    kept = copies(
        [(x_conv, x_out), (bc_conv, bc_out), (cums, cum_out), (deltas, delta_out)],
        sems.at[0:4],
    )
    for copy in kept:
        copy.start()
    last = cum[CHIP - 1 : CHIP, :]
    trailing = jnp.dot(jnp.exp(last - cum) * delta, spread(), precision=EXACT, preferred_element_type=F32)
    weighted = (x_conv[...].astype(F32) * trailing).astype(BF16)
    added = lax.dot_general(
        weighted, bc_conv[:, 0:N], (((0,), (0,)), ((), ())), preferred_element_type=F32
    )
    high = last.astype(BF16).astype(F32)
    middle = (last - high).astype(BF16).astype(F32)
    low = last - high - middle
    line = lax.broadcasted_iota(jnp.int32, (16, N), 0)
    for h in range(HEADS):
        added_out[h, 0:P_SIZE, :] = added[h * P_SIZE : (h + 1) * P_SIZE].astype(BF16)
        terms = jnp.where(
            line == 0,
            jnp.broadcast_to(high[:, h : h + 1], (16, N)),
            jnp.where(
                line == 1,
                jnp.broadcast_to(middle[:, h : h + 1], (16, N)),
                jnp.where(line == 2, jnp.broadcast_to(low[:, h : h + 1], (16, N)), 0.0),
            ),
        )
        added_out[h, P_SIZE : P_SIZE + 16, :] = terms.astype(BF16)
    for copy in kept:
        copy.wait()


def inside_kernel(
    x_in, bc_in, cum_in, delta_in, skip_in, zs, got,
    out, scale_out, x, bc, cum, delta, skip, gate, total, scales, sems,
):
    core, _ = place()
    fetch(
        [
            (x_in, x),
            (bc_in, bc),
            (cum_in, cum),
            (delta_in, delta),
            (skip_in, skip),
            (zs.at[:, lanes(core)], gate.at[tokens(core), :]),
            (got.at[:, 1152:1664], gate.at[tokens(1 - core), :]),
        ],
        sems,
    )
    decays = jnp.dot(jnp.exp(cum[...]), spread(), precision=EXACT, preferred_element_type=F32)
    gates = silu(gate[...].astype(F32))
    scales[...] = decays * gates
    scores = lax.dot_general(
        bc[:, N : 2 * N], bc[:, 0:N], (((1,), (1,)), ((), ())), preferred_element_type=F32
    )
    row = lax.broadcasted_iota(jnp.int32, (CHIP, CHIP), 0)
    column = lax.broadcasted_iota(jnp.int32, (CHIP, CHIP), 1)
    scores = jnp.where(row >= column, scores, 0.0)
    cum_t = jnp.transpose(cum[...])
    delta_t = jnp.transpose(delta[...])
    lane = lax.broadcasted_iota(jnp.int32, (CHIP, 128), 1)
    for pair in range(HEADS // 2):
        cut = slice(pair * 128, pair * 128 + 128)
        values = x[:, cut]
        both = []
        for h in (2 * pair, 2 * pair + 1):
            decay = jnp.exp(jnp.minimum(cum[:, h : h + 1] - cum_t[h : h + 1, :], 0.0))
            weights = (decay * scores * delta_t[h : h + 1, :]).astype(BF16)
            skips = jnp.where(core == 0, skip[:, h : h + 1], skip[:, HEADS + h : HEADS + h + 1])
            through = skips * values.astype(F32)
            both.append(jnp.dot(weights, values, preferred_element_type=F32) + through)
        total[:, cut] = jnp.where(lane < P_SIZE, both[0], both[1]) * gates[:, cut]
    fetch([(total, out), (scales, scale_out)], sems)


def prefix_kernel(got, first, out):
    state = first[...]
    for chip in range(CHIPS):
        out[chip] = state.astype(BF16)
        if chip < CHIPS - 1:
            terms = got[chip, P_SIZE : P_SIZE + 16, :].astype(F32)
            decay = jnp.exp(terms[0:1] + terms[1:2] + terms[2:3])
            state = decay * state + got[chip, 0:P_SIZE, :].astype(F32)


def carry_kernel(
    state_in, bc_in, inside_in, scale_in, gain_in,
    keep, to_core, to_next, to_cross, state, c, inside, scale, gain, pieces, sems,
):
    core, _ = place()
    fetch(
        [
            (bc_in.at[:, N : 2 * N], c),
            (state_in, state),
            (inside_in, inside),
            (scale_in, scale),
            (gain_in, gain),
        ],
        sems,
    )
    carried = lax.dot_general(
        c[...], state[...], (((1,), (1,)), ((), ())), preferred_element_type=F32
    )
    gated = inside[...] + carried * scale[...]
    pieces[...] = gated.astype(BF16).reshape(2, 4, 2, 16, HALF)

    def piece(side, parity):
        return pieces[pl.ds(side, 1), :, pl.ds(parity, 1)].reshape(64, HALF)

    odd = lax.rem(lax.axis_index("tensor"), 2)
    whole = gain[:, lanes(core)]
    high = whole.astype(BF16).astype(F32)
    middle = (whole - high).astype(BF16).astype(F32)
    low = whole - high - middle
    line = lax.broadcasted_iota(jnp.int32, (16, HALF), 0)
    terms = jnp.where(line == 0, high, jnp.where(line == 1, middle, jnp.where(line == 2, low, 0.0)))
    for out, side, parity in (
        (keep, core, odd), (to_core, 1 - core, odd), (to_next, core, 1 - odd), (to_cross, 1 - core, 1 - odd),
    ):
        out[0:64, :] = piece(side, parity)
        out[64:80, :] = terms.astype(BF16)


def norm_kernel(cross_got, next_got, core_got, keep, out):
    core, _ = place()
    odd = lax.rem(lax.axis_index("tensor"), 2)
    for mine, came, position in ((keep, core_got, odd), (next_got, cross_got, 1 - odd)):
        values = [ref[0:64, :].astype(F32) for ref in (mine, came)]
        squares = jnp.sum(values[0] * values[0] + values[1] * values[1], axis=1, keepdims=True)
        factor = lax.rsqrt(squares * (1.0 / 1024.0) + 1e-05)
        for ref, value, side in ((mine, values[0], core), (came, values[1], 1 - core)):
            terms = ref[64:80, :].astype(F32)
            gain = terms[0:1] + terms[1:2] + terms[2:3]
            at = pl.ds(pl.multiple_of(position * 1024 + side * HALF, HALF), HALF)
            out[:, at] = (value * factor * gain).astype(BF16)


def stage_kernel(source, out, sems):
    fetch([(source.at[i], out.at[i]) for i in range(4)], sems)


def product_kernel(*refs):
    *blocks, weights, out, rows, result, sems = refs
    count = len(blocks)
    for r, block in enumerate(blocks):
        rows[r * 64 : (r + 1) * 64, :] = block[...]
    moving = []
    for side in range(2):
        value = jnp.dot(rows[:, 0:1024], weights[2 * side], preferred_element_type=F32)
        value = value + jnp.dot(rows[:, 1024:2048], weights[2 * side + 1], preferred_element_type=F32)
        value = value.astype(BF16)
        for r in range(count):
            result[side, :, r] = value[r * 64 : (r + 1) * 64].reshape(4, 16, HALF)
        copy = pltpu.make_async_copy(
            result.at[side], out.at[:, :, :, side * HALF : (side + 1) * HALF], sems.at[side]
        )
        copy.start()
        moving.append(copy)
    for copy in moving:
        copy.wait()


def product(blocks, weights):
    count = len(blocks)
    return call(
        product_kernel,
        shaped((4, count, 16, 1024), BF16),
        scratch=[
            pltpu.VMEM((count * 64, 2048), BF16),
            pltpu.VMEM((2, 4, count, 16, HALF), BF16),
            pltpu.SemaphoreType.DMA((2,)),
        ],
        in_specs=[VMEM] * (count + 1),
        out_specs=HBM,
        flops=count * 270_000_000,
        moved=6 << 20,
    )(*blocks, weights)


def summed_over(terms, unit):
    total = terms[0, unit].astype(F32)
    for source in range(1, 4):
        total = total + terms[source, unit].astype(F32)
    return total.astype(BF16)


def collect_kernel(near, far, out, summed, sems):
    _, chip = place()
    moving = copies([(near, summed)], sems)
    moving[0].start()
    for r, before in enumerate(FAR):
        out[lax.rem(chip + (CHIPS - before), CHIPS)] = summed_over(far, r)
    moving[0].wait()
    for r, before in enumerate(NEAR):
        out[lax.rem(chip + (CHIPS - before), CHIPS)] = summed[r]


def body(
    xs, bcs, zs, dt_raw, tail_x, tail_bc, conv_x, conv_bc,
    dt_bias, a_log, d_skip, init_state, norm_gain, out_weight,
):
    core, chip = place()
    weights = lax.all_gather(out_weight, "tensor", axis=0, tiled=True, axis_index_groups=BOTH)
    sent, halo_0, halo_1, mine, fixed = call(
        pack_kernel,
        (
            shaped((ROWS, 1664), BF16),
            shaped((16, 1024), BF16),
            shaped((16, 1024), BF16),
            shaped((ROWS, HALF), BF16),
            shaped((32, 1024), F32),
        ),
        scratch=[
            pltpu.VMEM((ROWS, 2, N), BF16),
            pltpu.VMEM((16, ROWS), BF16),
            pltpu.VMEM((3, 1024), BF16),
            pltpu.VMEM((3, 2, N), BF16),
            pltpu.VMEM((4, 1024), BF16),
            pltpu.VMEM((4, 2, N), BF16),
            pltpu.VMEM((1, 16), F32),
            pltpu.VMEM((1, 16), F32),
            pltpu.VMEM((2, 128), F32),
            pltpu.SemaphoreType.DMA((13,)),
        ],
        in_specs=[HBM] * 10,
        out_specs=[VMEM] * 5,
        moved=1 << 20,
        limit=WIDE,
    )(
        xs, zs, bcs, dt_raw.T, tail_x, tail_bc, conv_x, conv_bc,
        dt_bias.reshape(1, 16), a_log.reshape(1, 16),
    )
    got = lax.ppermute(sent, "context", PAIR)
    halo_0 = lax.ppermute(halo_0, "context", TO_CORE_0)
    halo_1 = lax.ppermute(halo_1, "context", TO_CORE_1)
    added, x_conv, bc_conv, cum, delta = call(
        conv_kernel,
        (
            shaped((HEADS, P_SIZE + 16, N), BF16),
            shaped((CHIP, HALF), BF16),
            shaped((CHIP, 512), BF16),
            shaped((CHIP, 128), F32),
            shaped((CHIP, 128), F32),
        ),
        scratch=[
            pltpu.VMEM((CHIP + 16, 1024), F32),
            pltpu.VMEM((CHIP, 128), F32),
            pltpu.VMEM((CHIP, HALF), BF16),
            pltpu.VMEM((CHIP, 512), BF16),
            pltpu.VMEM((CHIP, 128), F32),
            pltpu.VMEM((CHIP, 128), F32),
            pltpu.VMEM((ROWS, HALF), BF16),
            pltpu.VMEM((ROWS, 640), BF16),
            pltpu.VMEM((ROWS, 1152), BF16),
            pltpu.VMEM((16, 1024), BF16),
            pltpu.VMEM((16, 1024), BF16),
            pltpu.VMEM((32, 1024), F32),
            pltpu.SemaphoreType.DMA((10,)),
        ],
        in_specs=[HBM] * 6,
        out_specs=[VMEM] + [HBM] * 4,
        limit=WIDE,
        flops=200_000_000,
        moved=2 << 20,
    )(mine, sent, got, halo_0, halo_1, fixed)
    increments = lax.all_to_all(added, "context", 0, 0, tiled=True, axis_index_groups=SAME_CORE)
    inside, scale = call(
        inside_kernel,
        (shaped((CHIP, HALF), F32), shaped((CHIP, HALF), F32)),
        scratch=[
            pltpu.VMEM((CHIP, HALF), BF16),
            pltpu.VMEM((CHIP, 512), BF16),
            pltpu.VMEM((CHIP, 128), F32),
            pltpu.VMEM((CHIP, 128), F32),
            pltpu.VMEM((1, 16), F32),
            pltpu.VMEM((CHIP, HALF), BF16),
            pltpu.VMEM((CHIP, HALF), F32),
            pltpu.VMEM((CHIP, HALF), F32),
            pltpu.SemaphoreType.DMA((7,)),
        ],
        in_specs=[HBM] * 7,
        out_specs=[HBM] * 2,
        flops=400_000_000,
        moved=2 << 20,
        limit=WIDE,
    )(x_conv, bc_conv, cum, delta, d_skip.reshape(1, 16), zs, got)
    increments, inside = lax.optimization_barrier((increments, inside))
    first = lax.dynamic_index_in_dim(init_state, core * HEADS + chip, 0, keepdims=False)
    states = call(
        prefix_kernel,
        shaped((CHIPS, P_SIZE, N), BF16),
        in_specs=[VMEM] * 2,
        moved=1 << 20,
    )(increments, first)
    states = lax.all_to_all(states, "context", 0, 0, tiled=True, axis_index_groups=SAME_CORE)
    states, weights = lax.optimization_barrier((states, weights))
    weights = lax.all_gather(weights, "context", axis=0, tiled=True, axis_index_groups=CORES)
    weights = weights.reshape(4, 1024, HALF)
    gain = norm_gain.reshape(1, 1024)
    keep, to_core, to_next, to_cross = call(
        carry_kernel,
        (shaped((80, HALF), BF16),) * 4,
        scratch=[
            pltpu.VMEM((HEADS * P_SIZE, N), BF16),
            pltpu.VMEM((CHIP, N), BF16),
            pltpu.VMEM((CHIP, HALF), F32),
            pltpu.VMEM((CHIP, HALF), F32),
            pltpu.VMEM((1, 1024), F32),
            pltpu.VMEM((2, 4, 2, 16, HALF), BF16),
            pltpu.SemaphoreType.DMA((5,)),
        ],
        in_specs=[HBM] * 5,
        out_specs=[VMEM] * 4,
        limit=WIDE,
        flops=100_000_000,
        moved=2 << 20,
    )(states.reshape(HEADS * P_SIZE, N), bc_conv, inside, scale, gain)
    cross_got = lax.ppermute(to_cross, ("context", "tensor"), CROSS)
    next_got = lax.ppermute(to_next, "tensor", BESIDE)
    core_got = lax.ppermute(to_core, "context", PAIR)
    normed = call(
        norm_kernel,
        shaped((64, 2048), BF16),
        in_specs=[VMEM] * 4,
        out_specs=VMEM,
        moved=1 << 20,
    )(cross_got, next_got, core_got, keep)

    def staged(weights):
        return call(
            stage_kernel,
            shaped((4, 1024, HALF), BF16),
            scratch=[pltpu.SemaphoreType.DMA((4,))],
            in_specs=[HBM],
            out_specs=VMEM,
            moved=8 << 20,
            limit=48 * 1024 * 1024,
        )(weights)

    up, down = [normed], [normed]
    for step in range(4):
        if step == 1:
            up[1], weights = lax.optimization_barrier((up[1], weights))
        up.append(lax.ppermute(up[-1], "context", UP))
        if step < 3:
            down.append(lax.ppermute(down[-1], "context", DOWN))
    blocks = {**{r: up[r] for r in range(5)}, **{CHIPS - r: down[r] for r in range(1, 4)}}
    near = product([blocks[r] for r in NEAR], staged(weights))
    blocks[3], weights = lax.optimization_barrier((blocks[3], weights))
    far = product([blocks[r] for r in FAR], staged(weights))
    near = lax.psum_scatter(
        near.reshape(4 * 16 * len(NEAR), 1024), "tensor",
        scatter_dimension=0, tiled=True, axis_index_groups=PARITY,
    )
    far = lax.all_to_all(
        far.reshape(4, 16 * len(FAR), 1024), "tensor", 0, 0, tiled=True, axis_index_groups=PARITY
    )
    ready = call(
        collect_kernel,
        shaped((CHIPS, 16, 1024), BF16),
        scratch=[pltpu.VMEM((len(NEAR), 16, 1024), BF16), pltpu.SemaphoreType.DMA((1,))],
        in_specs=[HBM, VMEM],
        moved=2 << 20,
    )(near.reshape(len(NEAR), 16, 1024), far.reshape(4, len(FAR), 16, 1024))
    return lax.all_to_all(
        ready, "context", 0, 0, tiled=True, axis_index_groups=SAME_CORE
    ).transpose(1, 0, 2).reshape(16, 8192)


def solution(mesh):
    return jax.shard_map(
        body,
        mesh=mesh,
        in_specs=(
            P(("dp", "context"), "tensor"),
            P(("dp", "context"), None, "tensor"),
            P(("dp", "context"), "tensor"),
            P(("dp", "context"), "tensor"),
            P("dp", "tensor"),
            P("dp", None, "tensor"),
            P(None, "tensor"),
            P(None, None, "tensor"),
            P("tensor"),
            P("tensor"),
            P("tensor"),
            P(("dp", "tensor"), None, None),
            P("tensor"),
            P("tensor", "context"),
        ),
        out_specs=P(("dp", "context", "tensor"), None),
        check_vma=False,
    )
```

```python
import functools

import jax
import jax.numpy as jnp
from jax import lax
from jax.experimental import pallas as pl
from jax.experimental.pallas import tpu as pltpu
from jax.sharding import PartitionSpec as P

ROWS = 128
CHIP = 256
HALF = 512
HEADS = 8
P_SIZE = 64
N = 256
CHIPS = 8
PAIR = [(i, i ^ 1) for i in range(16)]
SAME_CORE = [[2 * i + k for i in range(CHIPS)] for k in range(2)]
UP = [(i, (i + 2) % 16) for i in range(16)]
DOWN = [(i, (i - 2) % 16) for i in range(16)]
CROSS = [(8 * i + t, 8 * (i ^ 1) + (t ^ 1)) for i in range(16) for t in range(8)]
BESIDE = [(t, t ^ 1) for t in range(8)]
PARITY = [[0, 2, 4, 6], [1, 3, 5, 7]]
CORES = [[2 * i, 2 * i + 1] for i in range(CHIPS)]
BOTH = [[0, 1], [2, 3], [4, 5], [6, 7]]
NEAR = (0, 1, 7, 6, 2)
FAR = (3, 5, 4)
TO_CORE_0 = [(2 * i + 1, 2 * i + 2) for i in range(CHIPS - 1)]
TO_CORE_1 = [(2 * i + 1, 2 * i + 3) for i in range(CHIPS - 1)]
F32 = jnp.float32
BF16 = jnp.bfloat16
EXACT = lax.Precision.HIGHEST
LIMIT = 24 * 1024 * 1024
WIDE = 63 * 1024 * 1024


def call(kernel, out_shape, scratch=(), flops=0, moved=0, limit=LIMIT, **kwargs):
    return pl.pallas_call(
        kernel,
        out_shape=out_shape,
        scratch_shapes=list(scratch),
        compiler_params=pltpu.CompilerParams(vmem_limit_bytes=limit),
        cost_estimate=pl.CostEstimate(flops=flops, bytes_accessed=moved, transcendentals=0),
        **kwargs,
    )


VMEM = pl.BlockSpec(memory_space=pltpu.VMEM)
HBM = pl.BlockSpec(memory_space=pltpu.HBM)


def shaped(shape, dtype):
    return jax.ShapeDtypeStruct(shape, dtype)


def silu(v):
    return v / (1.0 + jnp.exp(-v))


def half_of(ref, core):
    return ref[:, pl.ds(pl.multiple_of(core * HALF, HALF), HALF)]


def spread():
    head = lax.broadcasted_iota(jnp.int32, (128, HALF), 0)
    lane = lax.broadcasted_iota(jnp.int32, (128, HALF), 1)
    return (lane // P_SIZE == head).astype(F32)


def place():
    position = lax.axis_index("context")
    return lax.rem(position, 2), lax.div(position, 2)


def copies(pairs, sems):
    return [pltpu.make_async_copy(source, target, sems.at[i]) for i, (source, target) in enumerate(pairs)]


def fetch(pairs, sems):
    moving = copies(pairs, sems)
    for copy in moving:
        copy.start()
    for copy in moving:
        copy.wait()


def lanes(core):
    return pl.ds(pl.multiple_of(core * HALF, HALF), HALF)


def tokens(core):
    return pl.ds(pl.multiple_of(core * ROWS, ROWS), ROWS)


TAPS, BIAS, RATE = 16, 20, 21


def pack_kernel(
    xs, zs, bcs, dt, tail_x, tail_bc, taps_x, taps_bc, bias, rate,
    send, halo_0, halo_1, mine, fixed, b_c, steps, tail_2, tail_3, taps_2, taps_3, bias_1, rate_1, heads, sems,
):
    core, _ = place()
    heads[...] = jnp.zeros((2, 128), F32)
    fetch(
        [
            (bcs, b_c),
            (dt, steps),
            (tail_x, tail_2),
            (tail_bc, tail_3),
            (taps_x, taps_2),
            (taps_bc, taps_3),
            (bias, bias_1),
            (rate, rate_1),
            (xs.at[:, lanes(1 - core)], send.at[:, 0:512]),
            (zs.at[:, lanes(1 - core)], send.at[:, 1152:1664]),
            (xs.at[:, lanes(core)], mine),
            (xs.at[112:128, 0:512], halo_0.at[:, 0:512]),
            (xs.at[112:128, 512:1024], halo_1.at[:, 0:512]),
        ],
        sems,
    )
    send[:, 512:768] = b_c[:, 0, :]
    send[:, 768:1024] = b_c[:, 1, :]
    by_head = jnp.concatenate([steps[...].astype(F32), jnp.zeros((112, ROWS), F32)], axis=0)
    send[:, 1024:1152] = jnp.transpose(by_head).astype(BF16)
    halo_0[:, 512:1024] = send[112:128, 512:1024]
    halo_1[:, 512:1024] = send[112:128, 512:1024]
    fixed[...] = jnp.zeros((32, 1024), F32)
    fixed[13:16, 0:512] = half_of(tail_2, core).astype(F32)
    fixed[13:16, 512:768] = tail_3[:, 0, :].astype(F32)
    fixed[13:16, 768:1024] = tail_3[:, 1, :].astype(F32)
    fixed[TAPS : TAPS + 4, 0:512] = half_of(taps_2, core).astype(F32)
    fixed[TAPS : TAPS + 4, 512:768] = taps_3[:, 0, :].astype(F32)
    fixed[TAPS : TAPS + 4, 768:1024] = taps_3[:, 1, :].astype(F32)
    heads[0:1, 0:16] = bias_1[...]
    heads[1:2, 0:16] = rate_1[...]
    own = jnp.where(core == 0, heads[...], pltpu.roll(heads[...], 120, 1))
    fixed[BIAS : BIAS + 1, 0:128] = own[0:1]
    fixed[RATE : RATE + 1, 0:128] = -jnp.exp(own[1:2])


def conv_kernel(
    xs_in, sent_in, got_in, halo_0_in, halo_1_in, fixed_in,
    added_out, x_out, bc_out, cum_out, delta_out, rows, steps, x_conv, bc_conv, cums, deltas,
    xs, sent, got, halo_0, halo_1, fixed, sems,
):
    core, chip = place()
    mine, other = tokens(core), tokens(1 - core)
    fetch(
        [
            (xs_in, xs),
            (sent_in.at[:, 512:1152], sent),
            (got_in.at[:, 0:1152], got),
            (halo_0_in, halo_0),
            (halo_1_in, halo_1),
            (fixed_in, fixed),
        ],
        sems.at[4:10],
    )
    first = pl.multiple_of(core * ROWS + 16, 16)
    second = pl.multiple_of((1 - core) * ROWS + 16, 16)
    rows[pl.ds(first, ROWS), 0:512] = xs[...].astype(F32)
    rows[pl.ds(first, ROWS), 512:1024] = sent[:, 0:512].astype(F32)
    rows[pl.ds(second, ROWS), :] = got[:, 0:1024].astype(F32)
    halo = halo_0[...].astype(F32) + halo_1[...].astype(F32)
    rows[0:16, :] = jnp.where(chip == 0, fixed[0:16, :], halo)
    for lane in range(0, 1024, 128):
        cut = slice(lane, lane + 128)
        total = fixed[TAPS : TAPS + 1, cut] * rows[13 : 13 + CHIP, cut]
        for k in range(1, 4):
            total = total + fixed[TAPS + k : TAPS + k + 1, cut] * rows[13 + k : 13 + k + CHIP, cut]
        value = silu(total).astype(BF16)
        if lane < 512:
            x_conv[:, cut] = value
        else:
            bc_conv[:, lane - 512 : lane - 384] = value
    steps[mine, :] = sent[:, 512:640].astype(F32)
    steps[other, :] = got[:, 1024:1152].astype(F32)
    raw = jnp.where(core == 0, steps[...], pltpu.roll(steps[...], 120, 1)) + fixed[BIAS : BIAS + 1, 0:128]
    delta = jnp.maximum(raw, 0.0) + jnp.log(1.0 + jnp.exp(-jnp.abs(raw)))
    logs = delta * fixed[RATE : RATE + 1, 0:128]
    row = lax.broadcasted_iota(jnp.int32, (CHIP, CHIP), 0)
    column = lax.broadcasted_iota(jnp.int32, (CHIP, CHIP), 1)
    cum = jnp.dot((row >= column).astype(F32), logs, precision=EXACT, preferred_element_type=F32)
    cums[...] = cum
    deltas[...] = delta
    kept = copies(
        [(x_conv, x_out), (bc_conv, bc_out), (cums, cum_out), (deltas, delta_out)],
        sems.at[0:4],
    )
    for copy in kept:
        copy.start()
    last = cum[CHIP - 1 : CHIP, :]
    trailing = jnp.dot(jnp.exp(last - cum) * delta, spread(), precision=EXACT, preferred_element_type=F32)
    weighted = (x_conv[...].astype(F32) * trailing).astype(BF16)
    added = lax.dot_general(
        weighted, bc_conv[:, 0:N], (((0,), (0,)), ((), ())), preferred_element_type=F32
    )
    high = last.astype(BF16).astype(F32)
    middle = (last - high).astype(BF16).astype(F32)
    low = last - high - middle
    line = lax.broadcasted_iota(jnp.int32, (16, N), 0)
    for h in range(HEADS):
        added_out[h, 0:P_SIZE, :] = added[h * P_SIZE : (h + 1) * P_SIZE].astype(BF16)
        terms = jnp.where(
            line == 0,
            jnp.broadcast_to(high[:, h : h + 1], (16, N)),
            jnp.where(
                line == 1,
                jnp.broadcast_to(middle[:, h : h + 1], (16, N)),
                jnp.where(line == 2, jnp.broadcast_to(low[:, h : h + 1], (16, N)), 0.0),
            ),
        )
        added_out[h, P_SIZE : P_SIZE + 16, :] = terms.astype(BF16)
    for copy in kept:
        copy.wait()


def inside_kernel(
    x_in, bc_in, cum_in, delta_in, skip_in, zs, got,
    out, scale_out, x, bc, cum, delta, skip, gate, total, scales, sems,
):
    core, _ = place()
    fetch(
        [
            (x_in, x),
            (bc_in, bc),
            (cum_in, cum),
            (delta_in, delta),
            (skip_in, skip),
            (zs.at[:, lanes(core)], gate.at[tokens(core), :]),
            (got.at[:, 1152:1664], gate.at[tokens(1 - core), :]),
        ],
        sems,
    )
    decays = jnp.dot(jnp.exp(cum[...]), spread(), precision=EXACT, preferred_element_type=F32)
    gates = silu(gate[...].astype(F32))
    scales[...] = decays * gates
    scores = lax.dot_general(
        bc[:, N : 2 * N], bc[:, 0:N], (((1,), (1,)), ((), ())), preferred_element_type=F32
    )
    row = lax.broadcasted_iota(jnp.int32, (CHIP, CHIP), 0)
    column = lax.broadcasted_iota(jnp.int32, (CHIP, CHIP), 1)
    scores = jnp.where(row >= column, scores, 0.0)
    cum_t = jnp.transpose(cum[...])
    delta_t = jnp.transpose(delta[...])
    lane = lax.broadcasted_iota(jnp.int32, (CHIP, 128), 1)
    for pair in range(HEADS // 2):
        cut = slice(pair * 128, pair * 128 + 128)
        values = x[:, cut]
        both = []
        for h in (2 * pair, 2 * pair + 1):
            decay = jnp.exp(jnp.minimum(cum[:, h : h + 1] - cum_t[h : h + 1, :], 0.0))
            weights = (decay * scores * delta_t[h : h + 1, :]).astype(BF16)
            skips = jnp.where(core == 0, skip[:, h : h + 1], skip[:, HEADS + h : HEADS + h + 1])
            through = skips * values.astype(F32)
            both.append(jnp.dot(weights, values, preferred_element_type=F32) + through)
        total[:, cut] = jnp.where(lane < P_SIZE, both[0], both[1]) * gates[:, cut]
    fetch([(total, out), (scales, scale_out)], sems)


def prefix_kernel(got, first, out):
    state = first[...]
    for chip in range(CHIPS):
        out[chip] = state.astype(BF16)
        if chip < CHIPS - 1:
            terms = got[chip, P_SIZE : P_SIZE + 16, :].astype(F32)
            decay = jnp.exp(terms[0:1] + terms[1:2] + terms[2:3])
            state = decay * state + got[chip, 0:P_SIZE, :].astype(F32)


def carry_kernel(
    state_in, bc_in, inside_in, scale_in, gain_in,
    keep, to_core, to_next, to_cross, state, c, inside, scale, gain, pieces, sems,
):
    core, _ = place()
    fetch(
        [
            (bc_in.at[:, N : 2 * N], c),
            (state_in, state),
            (inside_in, inside),
            (scale_in, scale),
            (gain_in, gain),
        ],
        sems,
    )
    carried = lax.dot_general(
        c[...], state[...], (((1,), (1,)), ((), ())), preferred_element_type=F32
    )
    gated = inside[...] + carried * scale[...]
    pieces[...] = gated.astype(BF16).reshape(2, 4, 2, 16, HALF)

    def piece(side, parity):
        return pieces[pl.ds(side, 1), :, pl.ds(parity, 1)].reshape(64, HALF)

    odd = lax.rem(lax.axis_index("tensor"), 2)
    whole = gain[:, lanes(core)]
    high = whole.astype(BF16).astype(F32)
    middle = (whole - high).astype(BF16).astype(F32)
    low = whole - high - middle
    line = lax.broadcasted_iota(jnp.int32, (16, HALF), 0)
    terms = jnp.where(line == 0, high, jnp.where(line == 1, middle, jnp.where(line == 2, low, 0.0)))
    for out, side, parity in (
        (keep, core, odd), (to_core, 1 - core, odd), (to_next, core, 1 - odd), (to_cross, 1 - core, 1 - odd),
    ):
        out[0:64, :] = piece(side, parity)
        out[64:80, :] = terms.astype(BF16)


def norm_kernel(cross_got, next_got, core_got, keep, out):
    core, _ = place()
    odd = lax.rem(lax.axis_index("tensor"), 2)
    for mine, came, position in ((keep, core_got, odd), (next_got, cross_got, 1 - odd)):
        values = [ref[0:64, :].astype(F32) for ref in (mine, came)]
        squares = jnp.sum(values[0] * values[0] + values[1] * values[1], axis=1, keepdims=True)
        factor = lax.rsqrt(squares * (1.0 / 1024.0) + 1e-05)
        for ref, value, side in ((mine, values[0], core), (came, values[1], 1 - core)):
            terms = ref[64:80, :].astype(F32)
            gain = terms[0:1] + terms[1:2] + terms[2:3]
            at = pl.ds(pl.multiple_of(position * 1024 + side * HALF, HALF), HALF)
            out[:, at] = (value * factor * gain).astype(BF16)


def stage_kernel(source, out, sems):
    fetch([(source.at[i], out.at[i]) for i in range(4)], sems)


def product_kernel(first, held, *refs):
    *blocks, weights, out, rows, result, sems = refs[held:]
    count = len(blocks)
    for r, block in enumerate(blocks):
        rows[r * 64 : (r + 1) * 64, :] = block[...]
    moving = []
    for side in range(2):
        value = jnp.dot(rows[:, 0:1024], weights[2 * side], preferred_element_type=F32)
        value = value + jnp.dot(rows[:, 1024:2048], weights[2 * side + 1], preferred_element_type=F32)
        value = value.astype(BF16)
        for r in range(count):
            result[side, :, r] = value[r * 64 : (r + 1) * 64].reshape(4, 16, HALF)
        copy = pltpu.make_async_copy(
            result.at[side],
            out.at[:, first : first + count, :, side * HALF : (side + 1) * HALF],
            sems.at[side],
        )
        copy.start()
        moving.append(copy)
    for copy in moving:
        copy.wait()


def product(blocks, weights, units, first=0, held=None):
    count = len(blocks)
    kept = [] if held is None else [held]
    return call(
        functools.partial(product_kernel, first, len(kept)),
        shaped((4, units, 16, 1024), BF16),
        scratch=[
            pltpu.VMEM((count * 64, 2048), BF16),
            pltpu.VMEM((2, 4, count, 16, HALF), BF16),
            pltpu.SemaphoreType.DMA((2,)),
        ],
        in_specs=[HBM] * len(kept) + [VMEM] * (count + 1),
        out_specs=HBM,
        flops=count * 270_000_000,
        moved=6 << 20,
        input_output_aliases={0: 0} if kept else {},
    )(*kept, *blocks, weights)


def summed_over(terms, unit):
    total = terms[0, unit].astype(F32)
    for source in range(1, 4):
        total = total + terms[source, unit].astype(F32)
    return total.astype(BF16)


def collect_kernel(near, far, out, summed, sems):
    _, chip = place()
    moving = copies([(near, summed)], sems)
    moving[0].start()
    for r, before in enumerate(FAR):
        out[lax.rem(chip + (CHIPS - before), CHIPS)] = summed_over(far, r)
    moving[0].wait()
    for r, before in enumerate(NEAR):
        out[lax.rem(chip + (CHIPS - before), CHIPS)] = summed[r]


def body(
    xs, bcs, zs, dt_raw, tail_x, tail_bc, conv_x, conv_bc,
    dt_bias, a_log, d_skip, init_state, norm_gain, out_weight,
):
    core, chip = place()
    weights = lax.all_gather(out_weight, "tensor", axis=0, tiled=True, axis_index_groups=BOTH)
    sent, halo_0, halo_1, mine, fixed = call(
        pack_kernel,
        (
            shaped((ROWS, 1664), BF16),
            shaped((16, 1024), BF16),
            shaped((16, 1024), BF16),
            shaped((ROWS, HALF), BF16),
            shaped((32, 1024), F32),
        ),
        scratch=[
            pltpu.VMEM((ROWS, 2, N), BF16),
            pltpu.VMEM((16, ROWS), BF16),
            pltpu.VMEM((3, 1024), BF16),
            pltpu.VMEM((3, 2, N), BF16),
            pltpu.VMEM((4, 1024), BF16),
            pltpu.VMEM((4, 2, N), BF16),
            pltpu.VMEM((1, 16), F32),
            pltpu.VMEM((1, 16), F32),
            pltpu.VMEM((2, 128), F32),
            pltpu.SemaphoreType.DMA((13,)),
        ],
        in_specs=[HBM] * 10,
        out_specs=[VMEM] * 5,
        moved=1 << 20,
        limit=WIDE,
    )(
        xs, zs, bcs, dt_raw.T, tail_x, tail_bc, conv_x, conv_bc,
        dt_bias.reshape(1, 16), a_log.reshape(1, 16),
    )
    got = lax.ppermute(sent, "context", PAIR)
    halo_0 = lax.ppermute(halo_0, "context", TO_CORE_0)
    halo_1 = lax.ppermute(halo_1, "context", TO_CORE_1)
    added, x_conv, bc_conv, cum, delta = call(
        conv_kernel,
        (
            shaped((HEADS, P_SIZE + 16, N), BF16),
            shaped((CHIP, HALF), BF16),
            shaped((CHIP, 512), BF16),
            shaped((CHIP, 128), F32),
            shaped((CHIP, 128), F32),
        ),
        scratch=[
            pltpu.VMEM((CHIP + 16, 1024), F32),
            pltpu.VMEM((CHIP, 128), F32),
            pltpu.VMEM((CHIP, HALF), BF16),
            pltpu.VMEM((CHIP, 512), BF16),
            pltpu.VMEM((CHIP, 128), F32),
            pltpu.VMEM((CHIP, 128), F32),
            pltpu.VMEM((ROWS, HALF), BF16),
            pltpu.VMEM((ROWS, 640), BF16),
            pltpu.VMEM((ROWS, 1152), BF16),
            pltpu.VMEM((16, 1024), BF16),
            pltpu.VMEM((16, 1024), BF16),
            pltpu.VMEM((32, 1024), F32),
            pltpu.SemaphoreType.DMA((10,)),
        ],
        in_specs=[HBM] * 6,
        out_specs=[VMEM] + [HBM] * 4,
        limit=WIDE,
        flops=200_000_000,
        moved=2 << 20,
    )(mine, sent, got, halo_0, halo_1, fixed)
    increments = lax.all_to_all(added, "context", 0, 0, tiled=True, axis_index_groups=SAME_CORE)
    inside, scale = call(
        inside_kernel,
        (shaped((CHIP, HALF), F32), shaped((CHIP, HALF), F32)),
        scratch=[
            pltpu.VMEM((CHIP, HALF), BF16),
            pltpu.VMEM((CHIP, 512), BF16),
            pltpu.VMEM((CHIP, 128), F32),
            pltpu.VMEM((CHIP, 128), F32),
            pltpu.VMEM((1, 16), F32),
            pltpu.VMEM((CHIP, HALF), BF16),
            pltpu.VMEM((CHIP, HALF), F32),
            pltpu.VMEM((CHIP, HALF), F32),
            pltpu.SemaphoreType.DMA((7,)),
        ],
        in_specs=[HBM] * 7,
        out_specs=[HBM] * 2,
        flops=400_000_000,
        moved=2 << 20,
        limit=WIDE,
    )(x_conv, bc_conv, cum, delta, d_skip.reshape(1, 16), zs, got)
    increments, inside = lax.optimization_barrier((increments, inside))
    first = lax.dynamic_index_in_dim(init_state, core * HEADS + chip, 0, keepdims=False)
    states = call(
        prefix_kernel,
        shaped((CHIPS, P_SIZE, N), BF16),
        in_specs=[VMEM] * 2,
        moved=1 << 20,
    )(increments, first)
    states = lax.all_to_all(states, "context", 0, 0, tiled=True, axis_index_groups=SAME_CORE)
    states, weights = lax.optimization_barrier((states, weights))
    weights = lax.all_gather(weights, "context", axis=0, tiled=True, axis_index_groups=CORES)
    weights = weights.reshape(4, 1024, HALF)
    gain = norm_gain.reshape(1, 1024)
    keep, to_core, to_next, to_cross = call(
        carry_kernel,
        (shaped((80, HALF), BF16),) * 4,
        scratch=[
            pltpu.VMEM((HEADS * P_SIZE, N), BF16),
            pltpu.VMEM((CHIP, N), BF16),
            pltpu.VMEM((CHIP, HALF), F32),
            pltpu.VMEM((CHIP, HALF), F32),
            pltpu.VMEM((1, 1024), F32),
            pltpu.VMEM((2, 4, 2, 16, HALF), BF16),
            pltpu.SemaphoreType.DMA((5,)),
        ],
        in_specs=[HBM] * 5,
        out_specs=[VMEM] * 4,
        limit=WIDE,
        flops=100_000_000,
        moved=2 << 20,
    )(states.reshape(HEADS * P_SIZE, N), bc_conv, inside, scale, gain)
    cross_got = lax.ppermute(to_cross, ("context", "tensor"), CROSS)
    next_got = lax.ppermute(to_next, "tensor", BESIDE)
    core_got = lax.ppermute(to_core, "context", PAIR)
    normed = call(
        norm_kernel,
        shaped((64, 2048), BF16),
        in_specs=[VMEM] * 4,
        out_specs=VMEM,
        moved=1 << 20,
    )(cross_got, next_got, core_got, keep)

    def staged(weights):
        return call(
            stage_kernel,
            shaped((4, 1024, HALF), BF16),
            scratch=[pltpu.SemaphoreType.DMA((4,))],
            in_specs=[HBM],
            out_specs=VMEM,
            moved=8 << 20,
            limit=48 * 1024 * 1024,
        )(weights)

    up, down = [normed], [normed]
    for step in range(4):
        if step == 1:
            up[1], weights = lax.optimization_barrier((up[1], weights))
        up.append(lax.ppermute(up[-1], "context", UP))
        if step < 3:
            down.append(lax.ppermute(down[-1], "context", DOWN))
    blocks = {**{r: up[r] for r in range(5)}, **{CHIPS - r: down[r] for r in range(1, 4)}}
    near_weights = staged(weights)
    near = product([blocks[r] for r in NEAR[:-1]], near_weights, len(NEAR))
    near = product([blocks[NEAR[-1]]], near_weights, len(NEAR), len(NEAR) - 1, near)
    blocks[3], weights = lax.optimization_barrier((blocks[3], weights))
    far = product([blocks[r] for r in FAR], staged(weights), len(FAR))
    near = lax.psum_scatter(
        near.reshape(4 * 16 * len(NEAR), 1024), "tensor",
        scatter_dimension=0, tiled=True, axis_index_groups=PARITY,
    )
    far = lax.all_to_all(
        far.reshape(4, 16 * len(FAR), 1024), "tensor", 0, 0, tiled=True, axis_index_groups=PARITY
    )
    ready = call(
        collect_kernel,
        shaped((CHIPS, 16, 1024), BF16),
        scratch=[pltpu.VMEM((len(NEAR), 16, 1024), BF16), pltpu.SemaphoreType.DMA((1,))],
        in_specs=[HBM, VMEM],
        moved=2 << 20,
    )(near.reshape(len(NEAR), 16, 1024), far.reshape(4, len(FAR), 16, 1024))
    return lax.all_to_all(
        ready, "context", 0, 0, tiled=True, axis_index_groups=SAME_CORE
    ).transpose(1, 0, 2).reshape(16, 8192)


def solution(mesh):
    return jax.shard_map(
        body,
        mesh=mesh,
        in_specs=(
            P(("dp", "context"), "tensor"),
            P(("dp", "context"), None, "tensor"),
            P(("dp", "context"), "tensor"),
            P(("dp", "context"), "tensor"),
            P("dp", "tensor"),
            P("dp", None, "tensor"),
            P(None, "tensor"),
            P(None, None, "tensor"),
            P("tensor"),
            P("tensor"),
            P("tensor"),
            P(("dp", "tensor"), None, None),
            P("tensor"),
            P("tensor", "context"),
        ),
        out_specs=P(("dp", "context", "tensor"), None),
        check_vma=False,
    )
```

```python
import functools

import jax
import jax.numpy as jnp
from jax import lax
from jax.experimental import pallas as pl
from jax.experimental.pallas import tpu as pltpu
from jax.sharding import PartitionSpec as P

ROWS = 128
CHIP = 256
HALF = 512
HEADS = 8
P_SIZE = 64
N = 256
CHIPS = 8
PAIR = [(i, i ^ 1) for i in range(16)]
SAME_CORE = [[2 * i + k for i in range(CHIPS)] for k in range(2)]
BACKWARD = [group[::-1] for group in SAME_CORE]
UP = [(i, (i + 2) % 16) for i in range(16)]
DOWN = [(i, (i - 2) % 16) for i in range(16)]
CROSS = [(8 * i + t, 8 * (i ^ 1) + (t ^ 1)) for i in range(16) for t in range(8)]
BESIDE = [(t, t ^ 1) for t in range(8)]
PARITY = [[0, 2, 4, 6], [1, 3, 5, 7]]
CORES = [[2 * i, 2 * i + 1] for i in range(CHIPS)]
BOTH = [[0, 1], [2, 3], [4, 5], [6, 7]]
NEAR = (0, 1, 7, 6, 2)
FAR = (3, 5, 4)
TO_CORE_0 = [(2 * i + 1, 2 * i + 2) for i in range(CHIPS - 1)]
TO_CORE_1 = [(2 * i + 1, 2 * i + 3) for i in range(CHIPS - 1)]
F32 = jnp.float32
BF16 = jnp.bfloat16
EXACT = lax.Precision.HIGHEST
LIMIT = 24 * 1024 * 1024
WIDE = 63 * 1024 * 1024


def call(kernel, out_shape, scratch=(), flops=0, moved=0, limit=LIMIT, **kwargs):
    return pl.pallas_call(
        kernel,
        out_shape=out_shape,
        scratch_shapes=list(scratch),
        compiler_params=pltpu.CompilerParams(vmem_limit_bytes=limit),
        cost_estimate=pl.CostEstimate(flops=flops, bytes_accessed=moved, transcendentals=0),
        **kwargs,
    )


VMEM = pl.BlockSpec(memory_space=pltpu.VMEM)
HBM = pl.BlockSpec(memory_space=pltpu.HBM)


def shaped(shape, dtype):
    return jax.ShapeDtypeStruct(shape, dtype)


def silu(v):
    return v / (1.0 + jnp.exp(-v))


def half_of(ref, core):
    return ref[:, pl.ds(pl.multiple_of(core * HALF, HALF), HALF)]


def spread():
    head = lax.broadcasted_iota(jnp.int32, (128, HALF), 0)
    lane = lax.broadcasted_iota(jnp.int32, (128, HALF), 1)
    return (lane // P_SIZE == head).astype(F32)


def place():
    position = lax.axis_index("context")
    return lax.rem(position, 2), lax.div(position, 2)


def copies(pairs, sems):
    return [pltpu.make_async_copy(source, target, sems.at[i]) for i, (source, target) in enumerate(pairs)]


def fetch(pairs, sems):
    moving = copies(pairs, sems)
    for copy in moving:
        copy.start()
    for copy in moving:
        copy.wait()


def lanes(core):
    return pl.ds(pl.multiple_of(core * HALF, HALF), HALF)


def tokens(core):
    return pl.ds(pl.multiple_of(core * ROWS, ROWS), ROWS)


TAPS, BIAS, RATE = 16, 20, 21


def pack_kernel(
    xs, zs, bcs, dt, tail_x, tail_bc, taps_x, taps_bc, bias, rate,
    send, halo_0, halo_1, mine, fixed, b_c, steps, tail_2, tail_3, taps_2, taps_3, bias_1, rate_1, heads, sems,
):
    core, _ = place()
    heads[...] = jnp.zeros((2, 128), F32)
    fetch(
        [
            (bcs, b_c),
            (dt, steps),
            (tail_x, tail_2),
            (tail_bc, tail_3),
            (taps_x, taps_2),
            (taps_bc, taps_3),
            (bias, bias_1),
            (rate, rate_1),
            (xs.at[:, lanes(1 - core)], send.at[:, 0:512]),
            (zs.at[:, lanes(1 - core)], send.at[:, 1152:1664]),
            (xs.at[:, lanes(core)], mine),
            (xs.at[112:128, 0:512], halo_0.at[:, 0:512]),
            (xs.at[112:128, 512:1024], halo_1.at[:, 0:512]),
        ],
        sems,
    )
    send[:, 512:768] = b_c[:, 0, :]
    send[:, 768:1024] = b_c[:, 1, :]
    by_head = jnp.concatenate([steps[...].astype(F32), jnp.zeros((112, ROWS), F32)], axis=0)
    send[:, 1024:1152] = jnp.transpose(by_head).astype(BF16)
    halo_0[:, 512:1024] = send[112:128, 512:1024]
    halo_1[:, 512:1024] = send[112:128, 512:1024]
    fixed[...] = jnp.zeros((32, 1024), F32)
    fixed[13:16, 0:512] = half_of(tail_2, core).astype(F32)
    fixed[13:16, 512:768] = tail_3[:, 0, :].astype(F32)
    fixed[13:16, 768:1024] = tail_3[:, 1, :].astype(F32)
    fixed[TAPS : TAPS + 4, 0:512] = half_of(taps_2, core).astype(F32)
    fixed[TAPS : TAPS + 4, 512:768] = taps_3[:, 0, :].astype(F32)
    fixed[TAPS : TAPS + 4, 768:1024] = taps_3[:, 1, :].astype(F32)
    heads[0:1, 0:16] = bias_1[...]
    heads[1:2, 0:16] = rate_1[...]
    own = jnp.where(core == 0, heads[...], pltpu.roll(heads[...], 120, 1))
    fixed[BIAS : BIAS + 1, 0:128] = own[0:1]
    fixed[RATE : RATE + 1, 0:128] = -jnp.exp(own[1:2])


def conv_kernel(
    xs_in, sent_in, got_in, halo_0_in, halo_1_in, fixed_in,
    added_out, x_out, bc_out, cum_out, delta_out, rows, steps, x_conv, bc_conv, cums, deltas,
    xs, sent, got, halo_0, halo_1, fixed, sems,
):
    core, chip = place()
    mine, other = tokens(core), tokens(1 - core)
    fetch(
        [
            (xs_in, xs),
            (sent_in.at[:, 512:1152], sent),
            (got_in.at[:, 0:1152], got),
            (halo_0_in, halo_0),
            (halo_1_in, halo_1),
            (fixed_in, fixed),
        ],
        sems.at[4:10],
    )
    first = pl.multiple_of(core * ROWS + 16, 16)
    second = pl.multiple_of((1 - core) * ROWS + 16, 16)
    rows[pl.ds(first, ROWS), 0:512] = xs[...].astype(F32)
    rows[pl.ds(first, ROWS), 512:1024] = sent[:, 0:512].astype(F32)
    rows[pl.ds(second, ROWS), :] = got[:, 0:1024].astype(F32)
    halo = halo_0[...].astype(F32) + halo_1[...].astype(F32)
    rows[0:16, :] = jnp.where(chip == 0, fixed[0:16, :], halo)
    for lane in range(0, 1024, 128):
        cut = slice(lane, lane + 128)
        total = fixed[TAPS : TAPS + 1, cut] * rows[13 : 13 + CHIP, cut]
        for k in range(1, 4):
            total = total + fixed[TAPS + k : TAPS + k + 1, cut] * rows[13 + k : 13 + k + CHIP, cut]
        value = silu(total).astype(BF16)
        if lane < 512:
            x_conv[:, cut] = value
        else:
            bc_conv[:, lane - 512 : lane - 384] = value
    steps[mine, :] = sent[:, 512:640].astype(F32)
    steps[other, :] = got[:, 1024:1152].astype(F32)
    raw = jnp.where(core == 0, steps[...], pltpu.roll(steps[...], 120, 1)) + fixed[BIAS : BIAS + 1, 0:128]
    delta = jnp.maximum(raw, 0.0) + jnp.log(1.0 + jnp.exp(-jnp.abs(raw)))
    logs = delta * fixed[RATE : RATE + 1, 0:128]
    row = lax.broadcasted_iota(jnp.int32, (CHIP, CHIP), 0)
    column = lax.broadcasted_iota(jnp.int32, (CHIP, CHIP), 1)
    cum = jnp.dot((row >= column).astype(F32), logs, precision=EXACT, preferred_element_type=F32)
    cums[...] = cum
    deltas[...] = delta
    kept = copies(
        [(x_conv, x_out), (bc_conv, bc_out), (cums, cum_out), (deltas, delta_out)],
        sems.at[0:4],
    )
    for copy in kept:
        copy.start()
    last = cum[CHIP - 1 : CHIP, :]
    trailing = jnp.dot(jnp.exp(last - cum) * delta, spread(), precision=EXACT, preferred_element_type=F32)
    weighted = (x_conv[...].astype(F32) * trailing).astype(BF16)
    added = lax.dot_general(
        weighted, bc_conv[:, 0:N], (((0,), (0,)), ((), ())), preferred_element_type=F32
    )
    high = last.astype(BF16).astype(F32)
    middle = (last - high).astype(BF16).astype(F32)
    low = last - high - middle
    line = lax.broadcasted_iota(jnp.int32, (16, N), 0)
    for h in range(HEADS):
        added_out[h, 0:P_SIZE, :] = added[h * P_SIZE : (h + 1) * P_SIZE].astype(BF16)
        terms = jnp.where(
            line == 0,
            jnp.broadcast_to(high[:, h : h + 1], (16, N)),
            jnp.where(
                line == 1,
                jnp.broadcast_to(middle[:, h : h + 1], (16, N)),
                jnp.where(line == 2, jnp.broadcast_to(low[:, h : h + 1], (16, N)), 0.0),
            ),
        )
        added_out[h, P_SIZE : P_SIZE + 16, :] = terms.astype(BF16)
    for copy in kept:
        copy.wait()


def inside_kernel(
    x_in, bc_in, cum_in, delta_in, skip_in, zs, got,
    out, scale_out, x, bc, cum, delta, skip, gate, total, scales, sems,
):
    core, _ = place()
    fetch(
        [
            (x_in, x),
            (bc_in, bc),
            (cum_in, cum),
            (delta_in, delta),
            (skip_in, skip),
            (zs.at[:, lanes(core)], gate.at[tokens(core), :]),
            (got.at[:, 1152:1664], gate.at[tokens(1 - core), :]),
        ],
        sems,
    )
    decays = jnp.dot(jnp.exp(cum[...]), spread(), precision=EXACT, preferred_element_type=F32)
    gates = silu(gate[...].astype(F32))
    scales[...] = decays * gates
    scores = lax.dot_general(
        bc[:, N : 2 * N], bc[:, 0:N], (((1,), (1,)), ((), ())), preferred_element_type=F32
    )
    row = lax.broadcasted_iota(jnp.int32, (CHIP, CHIP), 0)
    column = lax.broadcasted_iota(jnp.int32, (CHIP, CHIP), 1)
    scores = jnp.where(row >= column, scores, 0.0)
    cum_t = jnp.transpose(cum[...])
    delta_t = jnp.transpose(delta[...])
    lane = lax.broadcasted_iota(jnp.int32, (CHIP, 128), 1)
    for pair in range(HEADS // 2):
        cut = slice(pair * 128, pair * 128 + 128)
        values = x[:, cut]
        both = []
        for h in (2 * pair, 2 * pair + 1):
            decay = jnp.exp(jnp.minimum(cum[:, h : h + 1] - cum_t[h : h + 1, :], 0.0))
            weights = (decay * scores * delta_t[h : h + 1, :]).astype(BF16)
            skips = jnp.where(core == 0, skip[:, h : h + 1], skip[:, HEADS + h : HEADS + h + 1])
            through = skips * values.astype(F32)
            both.append(jnp.dot(weights, values, preferred_element_type=F32) + through)
        total[:, cut] = jnp.where(lane < P_SIZE, both[0], both[1]) * gates[:, cut]
    fetch([(total, out), (scales, scale_out)], sems)


def prefix_kernel(got, first, out):
    state = first[...]
    for chip in range(CHIPS):
        out[CHIPS - 1 - chip] = state.astype(BF16)
        if chip < CHIPS - 1:
            terms = got[chip, P_SIZE : P_SIZE + 16, :].astype(F32)
            decay = jnp.exp(terms[0:1] + terms[1:2] + terms[2:3])
            state = decay * state + got[chip, 0:P_SIZE, :].astype(F32)


def carry_kernel(
    state_in, bc_in, inside_in, scale_in, gain_in,
    keep, to_core, to_next, to_cross, state, c, inside, scale, gain, pieces, sems,
):
    core, _ = place()
    fetch(
        [
            (bc_in.at[:, N : 2 * N], c),
            (inside_in, inside),
            (scale_in, scale),
            (gain_in, gain),
        ]
        + [
            (state_in.at[(7 - h) * P_SIZE : (8 - h) * P_SIZE], state.at[h * P_SIZE : (h + 1) * P_SIZE])
            for h in range(HEADS)
        ],
        sems,
    )
    carried = lax.dot_general(
        c[...], state[...], (((1,), (1,)), ((), ())), preferred_element_type=F32
    )
    gated = inside[...] + carried * scale[...]
    pieces[...] = gated.astype(BF16).reshape(2, 4, 2, 16, HALF)

    def piece(side, parity):
        return pieces[pl.ds(side, 1), :, pl.ds(parity, 1)].reshape(64, HALF)

    odd = lax.rem(lax.axis_index("tensor"), 2)
    whole = gain[:, lanes(core)]
    high = whole.astype(BF16).astype(F32)
    middle = (whole - high).astype(BF16).astype(F32)
    low = whole - high - middle
    line = lax.broadcasted_iota(jnp.int32, (16, HALF), 0)
    terms = jnp.where(line == 0, high, jnp.where(line == 1, middle, jnp.where(line == 2, low, 0.0)))
    for out, side, parity in (
        (keep, core, odd), (to_core, 1 - core, odd), (to_next, core, 1 - odd), (to_cross, 1 - core, 1 - odd),
    ):
        out[0:64, :] = piece(side, parity)
        out[64:80, :] = terms.astype(BF16)


def norm_kernel(cross_got, next_got, core_got, keep, out):
    core, _ = place()
    odd = lax.rem(lax.axis_index("tensor"), 2)
    for mine, came, position in ((keep, core_got, odd), (next_got, cross_got, 1 - odd)):
        values = [ref[0:64, :].astype(F32) for ref in (mine, came)]
        squares = jnp.sum(values[0] * values[0] + values[1] * values[1], axis=1, keepdims=True)
        factor = lax.rsqrt(squares * (1.0 / 1024.0) + 1e-05)
        for ref, value, side in ((mine, values[0], core), (came, values[1], 1 - core)):
            terms = ref[64:80, :].astype(F32)
            gain = terms[0:1] + terms[1:2] + terms[2:3]
            at = pl.ds(pl.multiple_of(position * 1024 + side * HALF, HALF), HALF)
            out[:, at] = (value * factor * gain).astype(BF16)


def stage_kernel(source, out, sems):
    fetch([(source.at[i], out.at[i]) for i in range(4)], sems)


def product_kernel(first, held, *refs):
    *blocks, weights, out, rows, result, sems = refs[held:]
    count = len(blocks)
    for r, block in enumerate(blocks):
        rows[r * 64 : (r + 1) * 64, :] = block[...]
    moving = []
    for side in range(2):
        value = jnp.dot(rows[:, 0:1024], weights[2 * side], preferred_element_type=F32)
        value = value + jnp.dot(rows[:, 1024:2048], weights[2 * side + 1], preferred_element_type=F32)
        value = value.astype(BF16)
        for r in range(count):
            result[side, :, r] = value[r * 64 : (r + 1) * 64].reshape(4, 16, HALF)
        copy = pltpu.make_async_copy(
            result.at[side],
            out.at[:, first : first + count, :, side * HALF : (side + 1) * HALF],
            sems.at[side],
        )
        copy.start()
        moving.append(copy)
    for copy in moving:
        copy.wait()


def product(blocks, weights, units, first=0, held=None):
    count = len(blocks)
    kept = [] if held is None else [held]
    return call(
        functools.partial(product_kernel, first, len(kept)),
        shaped((4, units, 16, 1024), BF16),
        scratch=[
            pltpu.VMEM((count * 64, 2048), BF16),
            pltpu.VMEM((2, 4, count, 16, HALF), BF16),
            pltpu.SemaphoreType.DMA((2,)),
        ],
        in_specs=[HBM] * len(kept) + [VMEM] * (count + 1),
        out_specs=HBM,
        flops=count * 270_000_000,
        moved=6 << 20,
        input_output_aliases={0: 0} if kept else {},
    )(*kept, *blocks, weights)


def summed_over(terms, unit):
    total = terms[0, unit].astype(F32)
    for source in range(1, 4):
        total = total + terms[source, unit].astype(F32)
    return total.astype(BF16)


def collect_kernel(near, far, out, summed, sems):
    _, chip = place()
    moving = copies([(near, summed)], sems)
    moving[0].start()
    for r, before in enumerate(FAR):
        out[CHIPS - 1 - lax.rem(chip + (CHIPS - before), CHIPS)] = summed_over(far, r)
    moving[0].wait()
    for r, before in enumerate(NEAR):
        out[CHIPS - 1 - lax.rem(chip + (CHIPS - before), CHIPS)] = summed[r]


def body(
    xs, bcs, zs, dt_raw, tail_x, tail_bc, conv_x, conv_bc,
    dt_bias, a_log, d_skip, init_state, norm_gain, out_weight,
):
    core, chip = place()
    weights = lax.all_gather(out_weight, "tensor", axis=0, tiled=True, axis_index_groups=BOTH)
    sent, halo_0, halo_1, mine, fixed = call(
        pack_kernel,
        (
            shaped((ROWS, 1664), BF16),
            shaped((16, 1024), BF16),
            shaped((16, 1024), BF16),
            shaped((ROWS, HALF), BF16),
            shaped((32, 1024), F32),
        ),
        scratch=[
            pltpu.VMEM((ROWS, 2, N), BF16),
            pltpu.VMEM((16, ROWS), BF16),
            pltpu.VMEM((3, 1024), BF16),
            pltpu.VMEM((3, 2, N), BF16),
            pltpu.VMEM((4, 1024), BF16),
            pltpu.VMEM((4, 2, N), BF16),
            pltpu.VMEM((1, 16), F32),
            pltpu.VMEM((1, 16), F32),
            pltpu.VMEM((2, 128), F32),
            pltpu.SemaphoreType.DMA((13,)),
        ],
        in_specs=[HBM] * 10,
        out_specs=[VMEM] * 5,
        moved=1 << 20,
        limit=WIDE,
    )(
        xs, zs, bcs, dt_raw.T, tail_x, tail_bc, conv_x, conv_bc,
        dt_bias.reshape(1, 16), a_log.reshape(1, 16),
    )
    got = lax.ppermute(sent, "context", PAIR)
    halo_0 = lax.ppermute(halo_0, "context", TO_CORE_0)
    halo_1 = lax.ppermute(halo_1, "context", TO_CORE_1)
    added, x_conv, bc_conv, cum, delta = call(
        conv_kernel,
        (
            shaped((HEADS, P_SIZE + 16, N), BF16),
            shaped((CHIP, HALF), BF16),
            shaped((CHIP, 512), BF16),
            shaped((CHIP, 128), F32),
            shaped((CHIP, 128), F32),
        ),
        scratch=[
            pltpu.VMEM((CHIP + 16, 1024), F32),
            pltpu.VMEM((CHIP, 128), F32),
            pltpu.VMEM((CHIP, HALF), BF16),
            pltpu.VMEM((CHIP, 512), BF16),
            pltpu.VMEM((CHIP, 128), F32),
            pltpu.VMEM((CHIP, 128), F32),
            pltpu.VMEM((ROWS, HALF), BF16),
            pltpu.VMEM((ROWS, 640), BF16),
            pltpu.VMEM((ROWS, 1152), BF16),
            pltpu.VMEM((16, 1024), BF16),
            pltpu.VMEM((16, 1024), BF16),
            pltpu.VMEM((32, 1024), F32),
            pltpu.SemaphoreType.DMA((10,)),
        ],
        in_specs=[HBM] * 6,
        out_specs=[VMEM] + [HBM] * 4,
        limit=WIDE,
        flops=200_000_000,
        moved=2 << 20,
    )(mine, sent, got, halo_0, halo_1, fixed)
    increments = lax.all_to_all(added, "context", 0, 0, tiled=True, axis_index_groups=SAME_CORE)
    inside, scale = call(
        inside_kernel,
        (shaped((CHIP, HALF), F32), shaped((CHIP, HALF), F32)),
        scratch=[
            pltpu.VMEM((CHIP, HALF), BF16),
            pltpu.VMEM((CHIP, 512), BF16),
            pltpu.VMEM((CHIP, 128), F32),
            pltpu.VMEM((CHIP, 128), F32),
            pltpu.VMEM((1, 16), F32),
            pltpu.VMEM((CHIP, HALF), BF16),
            pltpu.VMEM((CHIP, HALF), F32),
            pltpu.VMEM((CHIP, HALF), F32),
            pltpu.SemaphoreType.DMA((7,)),
        ],
        in_specs=[HBM] * 7,
        out_specs=[HBM] * 2,
        flops=400_000_000,
        moved=2 << 20,
        limit=WIDE,
    )(x_conv, bc_conv, cum, delta, d_skip.reshape(1, 16), zs, got)
    increments, inside = lax.optimization_barrier((increments, inside))
    first = lax.dynamic_index_in_dim(init_state, core * HEADS + chip, 0, keepdims=False)
    states = call(
        prefix_kernel,
        shaped((CHIPS, P_SIZE, N), BF16),
        in_specs=[VMEM] * 2,
        moved=1 << 20,
    )(increments, first)
    states = lax.all_to_all(states, "context", 0, 0, tiled=True, axis_index_groups=BACKWARD)
    states, weights = lax.optimization_barrier((states, weights))
    weights = lax.all_gather(weights, "context", axis=0, tiled=True, axis_index_groups=CORES)
    weights = weights.reshape(4, 1024, HALF)
    gain = norm_gain.reshape(1, 1024)
    keep, to_core, to_next, to_cross = call(
        carry_kernel,
        (shaped((80, HALF), BF16),) * 4,
        scratch=[
            pltpu.VMEM((HEADS * P_SIZE, N), BF16),
            pltpu.VMEM((CHIP, N), BF16),
            pltpu.VMEM((CHIP, HALF), F32),
            pltpu.VMEM((CHIP, HALF), F32),
            pltpu.VMEM((1, 1024), F32),
            pltpu.VMEM((2, 4, 2, 16, HALF), BF16),
            pltpu.SemaphoreType.DMA((4 + HEADS,)),
        ],
        in_specs=[HBM] * 5,
        out_specs=[VMEM] * 4,
        limit=WIDE,
        flops=100_000_000,
        moved=2 << 20,
    )(states.reshape(HEADS * P_SIZE, N), bc_conv, inside, scale, gain)
    cross_got = lax.ppermute(to_cross, ("context", "tensor"), CROSS)
    next_got = lax.ppermute(to_next, "tensor", BESIDE)
    core_got = lax.ppermute(to_core, "context", PAIR)
    normed = call(
        norm_kernel,
        shaped((64, 2048), BF16),
        in_specs=[VMEM] * 4,
        out_specs=VMEM,
        moved=1 << 20,
    )(cross_got, next_got, core_got, keep)

    def staged(weights):
        return call(
            stage_kernel,
            shaped((4, 1024, HALF), BF16),
            scratch=[pltpu.SemaphoreType.DMA((4,))],
            in_specs=[HBM],
            out_specs=VMEM,
            moved=8 << 20,
            limit=48 * 1024 * 1024,
        )(weights)

    up, down = [normed], [normed]
    for step in range(4):
        if step == 1:
            up[1], weights = lax.optimization_barrier((up[1], weights))
        up.append(lax.ppermute(up[-1], "context", UP))
        if step < 3:
            down.append(lax.ppermute(down[-1], "context", DOWN))
    blocks = {**{r: up[r] for r in range(5)}, **{CHIPS - r: down[r] for r in range(1, 4)}}
    near_weights = staged(weights)
    near = product([blocks[r] for r in NEAR[:-1]], near_weights, len(NEAR))
    near = product([blocks[NEAR[-1]]], near_weights, len(NEAR), len(NEAR) - 1, near)
    blocks[3], weights = lax.optimization_barrier((blocks[3], weights))
    far = product([blocks[r] for r in FAR], staged(weights), len(FAR))
    near = lax.psum_scatter(
        near.reshape(4 * 16 * len(NEAR), 1024), "tensor",
        scatter_dimension=0, tiled=True, axis_index_groups=PARITY,
    )
    far = lax.all_to_all(
        far.reshape(4, 16 * len(FAR), 1024), "tensor", 0, 0, tiled=True, axis_index_groups=PARITY
    )
    ready = call(
        collect_kernel,
        shaped((CHIPS, 16, 1024), BF16),
        scratch=[pltpu.VMEM((len(NEAR), 16, 1024), BF16), pltpu.SemaphoreType.DMA((1,))],
        in_specs=[HBM, VMEM],
        moved=2 << 20,
    )(near.reshape(len(NEAR), 16, 1024), far.reshape(4, len(FAR), 16, 1024))
    return lax.all_to_all(
        ready, "context", 0, 0, tiled=True, axis_index_groups=BACKWARD
    )[::-1].transpose(1, 0, 2).reshape(16, 8192)


def solution(mesh):
    return jax.shard_map(
        body,
        mesh=mesh,
        in_specs=(
            P(("dp", "context"), "tensor"),
            P(("dp", "context"), None, "tensor"),
            P(("dp", "context"), "tensor"),
            P(("dp", "context"), "tensor"),
            P("dp", "tensor"),
            P("dp", None, "tensor"),
            P(None, "tensor"),
            P(None, None, "tensor"),
            P("tensor"),
            P("tensor"),
            P("tensor"),
            P(("dp", "tensor"), None, None),
            P("tensor"),
            P("tensor", "context"),
        ),
        out_specs=P(("dp", "context", "tensor"), None),
        check_vma=False,
    )
```

```python
import functools

import jax
import jax.numpy as jnp
from jax import lax
from jax.experimental import pallas as pl
from jax.experimental.pallas import tpu as pltpu
from jax.sharding import PartitionSpec as P

ROWS = 128
CHIP = 256
HALF = 512
HEADS = 8
P_SIZE = 64
N = 256
CHIPS = 8
PAIR = [(i, i ^ 1) for i in range(16)]
SAME_CORE = [[2 * i + k for i in range(CHIPS)] for k in range(2)]
BACKWARD = [group[::-1] for group in SAME_CORE]
UP = [(i, (i + 2) % 16) for i in range(16)]
DOWN = [(i, (i - 2) % 16) for i in range(16)]
CROSS = [(8 * i + t, 8 * (i ^ 1) + (t ^ 1)) for i in range(16) for t in range(8)]
BESIDE = [(t, t ^ 1) for t in range(8)]
PARITY = [[0, 2, 4, 6], [1, 3, 5, 7]]
CORES = [[2 * i, 2 * i + 1] for i in range(CHIPS)]
BOTH = [[0, 1], [2, 3], [4, 5], [6, 7]]
NEAR = (0, 1, 7, 6, 2)
FAR = (3, 5, 4)
TO_CORE_0 = [(2 * i + 1, 2 * i + 2) for i in range(CHIPS - 1)]
TO_CORE_1 = [(2 * i + 1, 2 * i + 3) for i in range(CHIPS - 1)]
F32 = jnp.float32
BF16 = jnp.bfloat16
EXACT = lax.Precision.HIGHEST
LIMIT = 24 * 1024 * 1024
WIDE = 63 * 1024 * 1024


def call(kernel, out_shape, scratch=(), flops=0, moved=0, limit=LIMIT, **kwargs):
    return pl.pallas_call(
        kernel,
        out_shape=out_shape,
        scratch_shapes=list(scratch),
        compiler_params=pltpu.CompilerParams(vmem_limit_bytes=limit),
        cost_estimate=pl.CostEstimate(flops=flops, bytes_accessed=moved, transcendentals=0),
        **kwargs,
    )


VMEM = pl.BlockSpec(memory_space=pltpu.VMEM)
HBM = pl.BlockSpec(memory_space=pltpu.HBM)


def shaped(shape, dtype):
    return jax.ShapeDtypeStruct(shape, dtype)


def silu(v):
    return v / (1.0 + jnp.exp(-v))


def half_of(ref, core):
    return ref[:, pl.ds(pl.multiple_of(core * HALF, HALF), HALF)]


def spread():
    head = lax.broadcasted_iota(jnp.int32, (128, HALF), 0)
    lane = lax.broadcasted_iota(jnp.int32, (128, HALF), 1)
    return (lane // P_SIZE == head).astype(F32)


def place():
    position = lax.axis_index("context")
    return lax.rem(position, 2), lax.div(position, 2)


def copies(pairs, sems):
    return [pltpu.make_async_copy(source, target, sems.at[i]) for i, (source, target) in enumerate(pairs)]


def fetch(pairs, sems):
    moving = copies(pairs, sems)
    for copy in moving:
        copy.start()
    for copy in moving:
        copy.wait()


def lanes(core):
    return pl.ds(pl.multiple_of(core * HALF, HALF), HALF)


def tokens(core):
    return pl.ds(pl.multiple_of(core * ROWS, ROWS), ROWS)


TAPS, BIAS, RATE = 16, 20, 21


def pack_kernel(
    xs, zs, bcs, dt, tail_x, tail_bc, taps_x, taps_bc, bias, rate,
    send, halo_0, halo_1, mine, fixed, b_c, steps, tail_2, tail_3, taps_2, taps_3, bias_1, rate_1, heads, sems,
):
    core, _ = place()
    heads[...] = jnp.zeros((2, 128), F32)
    fetch(
        [
            (bcs, b_c),
            (dt, steps),
            (tail_x, tail_2),
            (tail_bc, tail_3),
            (taps_x, taps_2),
            (taps_bc, taps_3),
            (bias, bias_1),
            (rate, rate_1),
            (xs.at[:, lanes(1 - core)], send.at[:, 0:512]),
            (zs.at[:, lanes(1 - core)], send.at[:, 1152:1664]),
            (xs.at[:, lanes(core)], mine),
            (xs.at[112:128, 0:512], halo_0.at[:, 0:512]),
            (xs.at[112:128, 512:1024], halo_1.at[:, 0:512]),
        ],
        sems,
    )
    send[:, 512:768] = b_c[:, 0, :]
    send[:, 768:1024] = b_c[:, 1, :]
    by_head = jnp.concatenate([steps[...].astype(F32), jnp.zeros((112, ROWS), F32)], axis=0)
    send[:, 1024:1152] = jnp.transpose(by_head).astype(BF16)
    halo_0[:, 512:1024] = send[112:128, 512:1024]
    halo_1[:, 512:1024] = send[112:128, 512:1024]
    fixed[...] = jnp.zeros((32, 1024), F32)
    fixed[13:16, 0:512] = half_of(tail_2, core).astype(F32)
    fixed[13:16, 512:768] = tail_3[:, 0, :].astype(F32)
    fixed[13:16, 768:1024] = tail_3[:, 1, :].astype(F32)
    fixed[TAPS : TAPS + 4, 0:512] = half_of(taps_2, core).astype(F32)
    fixed[TAPS : TAPS + 4, 512:768] = taps_3[:, 0, :].astype(F32)
    fixed[TAPS : TAPS + 4, 768:1024] = taps_3[:, 1, :].astype(F32)
    heads[0:1, 0:16] = bias_1[...]
    heads[1:2, 0:16] = rate_1[...]
    own = jnp.where(core == 0, heads[...], pltpu.roll(heads[...], 120, 1))
    fixed[BIAS : BIAS + 1, 0:128] = own[0:1]
    fixed[RATE : RATE + 1, 0:128] = -jnp.exp(own[1:2])


def conv_kernel(
    xs_in, sent_in, got_in, halo_0_in, halo_1_in, fixed_in,
    added_out, x_out, bc_out, cum_out, delta_out, rows, steps, x_conv, bc_conv, cums, deltas,
    xs, sent, got, halo_0, halo_1, fixed, sems,
):
    core, chip = place()
    mine, other = tokens(core), tokens(1 - core)
    fetch(
        [
            (xs_in, xs),
            (sent_in.at[:, 512:1152], sent),
            (got_in.at[:, 0:1152], got),
            (halo_0_in, halo_0),
            (halo_1_in, halo_1),
            (fixed_in, fixed),
        ],
        sems.at[4:10],
    )
    first = pl.multiple_of(core * ROWS + 16, 16)
    second = pl.multiple_of((1 - core) * ROWS + 16, 16)
    rows[pl.ds(first, ROWS), 0:512] = xs[...].astype(F32)
    rows[pl.ds(first, ROWS), 512:1024] = sent[:, 0:512].astype(F32)
    rows[pl.ds(second, ROWS), :] = got[:, 0:1024].astype(F32)
    halo = halo_0[...].astype(F32) + halo_1[...].astype(F32)
    rows[0:16, :] = jnp.where(chip == 0, fixed[0:16, :], halo)
    for lane in range(0, 1024, 128):
        cut = slice(lane, lane + 128)
        total = fixed[TAPS : TAPS + 1, cut] * rows[13 : 13 + CHIP, cut]
        for k in range(1, 4):
            total = total + fixed[TAPS + k : TAPS + k + 1, cut] * rows[13 + k : 13 + k + CHIP, cut]
        value = silu(total).astype(BF16)
        if lane < 512:
            x_conv[:, cut] = value
        else:
            bc_conv[:, lane - 512 : lane - 384] = value
    steps[mine, :] = sent[:, 512:640].astype(F32)
    steps[other, :] = got[:, 1024:1152].astype(F32)
    raw = jnp.where(core == 0, steps[...], pltpu.roll(steps[...], 120, 1)) + fixed[BIAS : BIAS + 1, 0:128]
    delta = jnp.maximum(raw, 0.0) + jnp.log(1.0 + jnp.exp(-jnp.abs(raw)))
    logs = delta * fixed[RATE : RATE + 1, 0:128]
    row = lax.broadcasted_iota(jnp.int32, (CHIP, CHIP), 0)
    column = lax.broadcasted_iota(jnp.int32, (CHIP, CHIP), 1)
    cum = jnp.dot((row >= column).astype(F32), logs, precision=EXACT, preferred_element_type=F32)
    cums[...] = cum
    deltas[...] = delta
    kept = copies(
        [(x_conv, x_out), (bc_conv, bc_out), (cums, cum_out), (deltas, delta_out)],
        sems.at[0:4],
    )
    for copy in kept:
        copy.start()
    last = cum[CHIP - 1 : CHIP, :]
    trailing = jnp.dot(jnp.exp(last - cum) * delta, spread(), precision=EXACT, preferred_element_type=F32)
    weighted = (x_conv[...].astype(F32) * trailing).astype(BF16)
    added = lax.dot_general(
        weighted, bc_conv[:, 0:N], (((0,), (0,)), ((), ())), preferred_element_type=F32
    )
    high = last.astype(BF16).astype(F32)
    middle = (last - high).astype(BF16).astype(F32)
    low = last - high - middle
    line = lax.broadcasted_iota(jnp.int32, (16, N), 0)
    for h in range(HEADS):
        added_out[h, 0:P_SIZE, :] = added[h * P_SIZE : (h + 1) * P_SIZE].astype(BF16)
        terms = jnp.where(
            line == 0,
            jnp.broadcast_to(high[:, h : h + 1], (16, N)),
            jnp.where(
                line == 1,
                jnp.broadcast_to(middle[:, h : h + 1], (16, N)),
                jnp.where(line == 2, jnp.broadcast_to(low[:, h : h + 1], (16, N)), 0.0),
            ),
        )
        added_out[h, P_SIZE : P_SIZE + 16, :] = terms.astype(BF16)
    for copy in kept:
        copy.wait()


def inside_kernel(
    x_in, bc_in, cum_in, delta_in, skip_in, zs, got,
    out, scale_out, x, bc, cum, delta, skip, gate, total, scales, sems,
):
    core, _ = place()
    fetch(
        [
            (x_in, x),
            (bc_in, bc),
            (cum_in, cum),
            (delta_in, delta),
            (skip_in, skip),
            (zs.at[:, lanes(core)], gate.at[tokens(core), :]),
            (got.at[:, 1152:1664], gate.at[tokens(1 - core), :]),
        ],
        sems,
    )
    decays = jnp.dot(jnp.exp(cum[...]), spread(), precision=EXACT, preferred_element_type=F32)
    gates = silu(gate[...].astype(F32))
    scales[...] = decays * gates
    scores = lax.dot_general(
        bc[:, N : 2 * N], bc[:, 0:N], (((1,), (1,)), ((), ())), preferred_element_type=F32
    )
    row = lax.broadcasted_iota(jnp.int32, (CHIP, CHIP), 0)
    column = lax.broadcasted_iota(jnp.int32, (CHIP, CHIP), 1)
    scores = jnp.where(row >= column, scores, 0.0)
    cum_t = jnp.transpose(cum[...])
    delta_t = jnp.transpose(delta[...])
    lane = lax.broadcasted_iota(jnp.int32, (CHIP, 128), 1)
    for pair in range(HEADS // 2):
        cut = slice(pair * 128, pair * 128 + 128)
        values = x[:, cut]
        both = []
        for h in (2 * pair, 2 * pair + 1):
            decay = jnp.exp(jnp.minimum(cum[:, h : h + 1] - cum_t[h : h + 1, :], 0.0))
            weights = (decay * scores * delta_t[h : h + 1, :]).astype(BF16)
            skips = jnp.where(core == 0, skip[:, h : h + 1], skip[:, HEADS + h : HEADS + h + 1])
            through = skips * values.astype(F32)
            both.append(jnp.dot(weights, values, preferred_element_type=F32) + through)
        total[:, cut] = jnp.where(lane < P_SIZE, both[0], both[1]) * gates[:, cut]
    fetch([(total, out), (scales, scale_out)], sems)


def prefix_kernel(got, first, out):
    state = first[...]
    for chip in range(CHIPS):
        out[CHIPS - 1 - chip] = state.astype(BF16)
        if chip < CHIPS - 1:
            terms = got[chip, P_SIZE : P_SIZE + 16, :].astype(F32)
            decay = jnp.exp(terms[0:1] + terms[1:2] + terms[2:3])
            state = decay * state + got[chip, 0:P_SIZE, :].astype(F32)


def carry_kernel(
    state_in, bc_in, inside_in, scale_in, gain_in,
    keep, to_core, to_next, to_cross, state, c, inside, scale, gain, pieces, sems,
):
    core, _ = place()
    fetch(
        [
            (bc_in.at[:, N : 2 * N], c),
            (inside_in, inside),
            (scale_in, scale),
            (gain_in, gain),
        ]
        + [
            (state_in.at[(7 - h) * P_SIZE : (8 - h) * P_SIZE], state.at[h * P_SIZE : (h + 1) * P_SIZE])
            for h in range(HEADS)
        ],
        sems,
    )
    carried = lax.dot_general(
        c[...], state[...], (((1,), (1,)), ((), ())), preferred_element_type=F32
    )
    gated = inside[...] + carried * scale[...]
    pieces[...] = gated.astype(BF16).reshape(2, 4, 2, 16, HALF)

    def piece(side, parity):
        return pieces[pl.ds(side, 1), :, pl.ds(parity, 1)].reshape(64, HALF)

    odd = lax.rem(lax.axis_index("tensor"), 2)
    whole = gain[:, lanes(core)]
    high = whole.astype(BF16).astype(F32)
    middle = (whole - high).astype(BF16).astype(F32)
    low = whole - high - middle
    line = lax.broadcasted_iota(jnp.int32, (16, HALF), 0)
    terms = jnp.where(line == 0, high, jnp.where(line == 1, middle, jnp.where(line == 2, low, 0.0)))
    for out, side, parity in (
        (keep, core, odd), (to_core, 1 - core, odd), (to_next, core, 1 - odd), (to_cross, 1 - core, 1 - odd),
    ):
        out[0:64, :] = piece(side, parity)
        out[64:80, :] = terms.astype(BF16)


def norm_kernel(cross_got, next_got, core_got, keep, out):
    core, _ = place()
    odd = lax.rem(lax.axis_index("tensor"), 2)
    for mine, came, position in ((keep, core_got, odd), (next_got, cross_got, 1 - odd)):
        values = [ref[0:64, :].astype(F32) for ref in (mine, came)]
        squares = jnp.sum(values[0] * values[0] + values[1] * values[1], axis=1, keepdims=True)
        factor = lax.rsqrt(squares * (1.0 / 1024.0) + 1e-05)
        for ref, value, side in ((mine, values[0], core), (came, values[1], 1 - core)):
            terms = ref[64:80, :].astype(F32)
            gain = terms[0:1] + terms[1:2] + terms[2:3]
            at = pl.ds(pl.multiple_of(position * 1024 + side * HALF, HALF), HALF)
            out[:, at] = (value * factor * gain).astype(BF16)


def stage_kernel(source, out, sems):
    fetch([(source.at[i], out.at[i]) for i in range(4)], sems)


def product_kernel(first, held, *refs):
    *blocks, weights, out, rows, result, sems = refs[held:]
    count = len(blocks)
    for r, block in enumerate(blocks):
        rows[r * 64 : (r + 1) * 64, :] = block[...]
    moving = []
    for side in range(2):
        value = jnp.dot(rows[:, 0:1024], weights[2 * side], preferred_element_type=F32)
        value = value + jnp.dot(rows[:, 1024:2048], weights[2 * side + 1], preferred_element_type=F32)
        value = value.astype(BF16)
        for r in range(count):
            result[side, :, r] = value[r * 64 : (r + 1) * 64].reshape(4, 16, HALF)
        copy = pltpu.make_async_copy(
            result.at[side],
            out.at[:, first : first + count, :, side * HALF : (side + 1) * HALF],
            sems.at[side],
        )
        copy.start()
        moving.append(copy)
    for copy in moving:
        copy.wait()


def product(blocks, weights, units, first=0, held=None):
    count = len(blocks)
    kept = [] if held is None else [held]
    return call(
        functools.partial(product_kernel, first, len(kept)),
        shaped((4, units, 16, 1024), BF16),
        scratch=[
            pltpu.VMEM((count * 64, 2048), BF16),
            pltpu.VMEM((2, 4, count, 16, HALF), BF16),
            pltpu.SemaphoreType.DMA((2,)),
        ],
        in_specs=[HBM] * len(kept) + [VMEM] * (count + 1),
        out_specs=HBM,
        flops=count * 270_000_000,
        moved=6 << 20,
        input_output_aliases={0: 0} if kept else {},
    )(*kept, *blocks, weights)


def summed_over(terms, unit):
    total = terms[0, unit].astype(F32)
    for source in range(1, 4):
        total = total + terms[source, unit].astype(F32)
    return total.astype(BF16)


def collect_kernel(near, far, out, summed, sems):
    _, chip = place()
    moving = copies([(near, summed)], sems)
    moving[0].start()
    for r, before in enumerate(FAR):
        out[CHIPS - 1 - lax.rem(chip + (CHIPS - before), CHIPS)] = summed_over(far, r)
    moving[0].wait()
    for r, before in enumerate(NEAR):
        out[CHIPS - 1 - lax.rem(chip + (CHIPS - before), CHIPS)] = summed[r]


def body(
    xs, bcs, zs, dt_raw, tail_x, tail_bc, conv_x, conv_bc,
    dt_bias, a_log, d_skip, init_state, norm_gain, out_weight,
):
    core, chip = place()
    weights = lax.all_gather(out_weight, "tensor", axis=0, tiled=True, axis_index_groups=BOTH)
    sent, halo_0, halo_1, mine, fixed = call(
        pack_kernel,
        (
            shaped((ROWS, 1664), BF16),
            shaped((16, 1024), BF16),
            shaped((16, 1024), BF16),
            shaped((ROWS, HALF), BF16),
            shaped((32, 1024), F32),
        ),
        scratch=[
            pltpu.VMEM((ROWS, 2, N), BF16),
            pltpu.VMEM((16, ROWS), BF16),
            pltpu.VMEM((3, 1024), BF16),
            pltpu.VMEM((3, 2, N), BF16),
            pltpu.VMEM((4, 1024), BF16),
            pltpu.VMEM((4, 2, N), BF16),
            pltpu.VMEM((1, 16), F32),
            pltpu.VMEM((1, 16), F32),
            pltpu.VMEM((2, 128), F32),
            pltpu.SemaphoreType.DMA((13,)),
        ],
        in_specs=[HBM] * 10,
        out_specs=[VMEM] * 5,
        moved=1 << 20,
        limit=WIDE,
    )(
        xs, zs, bcs, dt_raw.T, tail_x, tail_bc, conv_x, conv_bc,
        dt_bias.reshape(1, 16), a_log.reshape(1, 16),
    )
    got = lax.ppermute(sent, "context", PAIR)
    halo_0 = lax.ppermute(halo_0, "context", TO_CORE_0)
    halo_1 = lax.ppermute(halo_1, "context", TO_CORE_1)
    added, x_conv, bc_conv, cum, delta = call(
        conv_kernel,
        (
            shaped((HEADS, P_SIZE + 16, N), BF16),
            shaped((CHIP, HALF), BF16),
            shaped((CHIP, 512), BF16),
            shaped((CHIP, 128), F32),
            shaped((CHIP, 128), F32),
        ),
        scratch=[
            pltpu.VMEM((CHIP + 16, 1024), F32),
            pltpu.VMEM((CHIP, 128), F32),
            pltpu.VMEM((CHIP, HALF), BF16),
            pltpu.VMEM((CHIP, 512), BF16),
            pltpu.VMEM((CHIP, 128), F32),
            pltpu.VMEM((CHIP, 128), F32),
            pltpu.VMEM((ROWS, HALF), BF16),
            pltpu.VMEM((ROWS, 640), BF16),
            pltpu.VMEM((ROWS, 1152), BF16),
            pltpu.VMEM((16, 1024), BF16),
            pltpu.VMEM((16, 1024), BF16),
            pltpu.VMEM((32, 1024), F32),
            pltpu.SemaphoreType.DMA((10,)),
        ],
        in_specs=[HBM] * 6,
        out_specs=[VMEM] + [HBM] * 4,
        limit=WIDE,
        flops=200_000_000,
        moved=2 << 20,
    )(mine, sent, got, halo_0, halo_1, fixed)
    increments = lax.all_to_all(added, "context", 0, 0, tiled=True, axis_index_groups=SAME_CORE)
    inside, scale = call(
        inside_kernel,
        (shaped((CHIP, HALF), F32), shaped((CHIP, HALF), F32)),
        scratch=[
            pltpu.VMEM((CHIP, HALF), BF16),
            pltpu.VMEM((CHIP, 512), BF16),
            pltpu.VMEM((CHIP, 128), F32),
            pltpu.VMEM((CHIP, 128), F32),
            pltpu.VMEM((1, 16), F32),
            pltpu.VMEM((CHIP, HALF), BF16),
            pltpu.VMEM((CHIP, HALF), F32),
            pltpu.VMEM((CHIP, HALF), F32),
            pltpu.SemaphoreType.DMA((7,)),
        ],
        in_specs=[HBM] * 7,
        out_specs=[HBM] * 2,
        flops=400_000_000,
        moved=2 << 20,
        limit=WIDE,
    )(x_conv, bc_conv, cum, delta, d_skip.reshape(1, 16), zs, got)
    increments, inside = lax.optimization_barrier((increments, inside))
    first = lax.dynamic_index_in_dim(init_state, core * HEADS + chip, 0, keepdims=False)
    states = call(
        prefix_kernel,
        shaped((CHIPS, P_SIZE, N), BF16),
        in_specs=[VMEM] * 2,
        moved=1 << 20,
    )(increments, first)
    states = lax.all_to_all(states, "context", 0, 0, tiled=True, axis_index_groups=BACKWARD)
    states, weights = lax.optimization_barrier((states, weights))
    weights = lax.all_gather(weights, "context", axis=0, tiled=True, axis_index_groups=CORES)
    weights = weights.reshape(4, 1024, HALF)
    gain = norm_gain.reshape(1, 1024)
    keep, to_core, to_next, to_cross = call(
        carry_kernel,
        (shaped((80, HALF), BF16),) * 4,
        scratch=[
            pltpu.VMEM((HEADS * P_SIZE, N), BF16),
            pltpu.VMEM((CHIP, N), BF16),
            pltpu.VMEM((CHIP, HALF), F32),
            pltpu.VMEM((CHIP, HALF), F32),
            pltpu.VMEM((1, 1024), F32),
            pltpu.VMEM((2, 4, 2, 16, HALF), BF16),
            pltpu.SemaphoreType.DMA((4 + HEADS,)),
        ],
        in_specs=[HBM] * 5,
        out_specs=[VMEM] * 4,
        limit=WIDE,
        flops=100_000_000,
        moved=2 << 20,
    )(states.reshape(HEADS * P_SIZE, N), bc_conv, inside, scale, gain)
    cross_got = lax.ppermute(to_cross, ("context", "tensor"), CROSS)
    next_got = lax.ppermute(to_next, "tensor", BESIDE)
    core_got = lax.ppermute(to_core, "context", PAIR)
    normed = call(
        norm_kernel,
        shaped((64, 2048), BF16),
        in_specs=[VMEM] * 4,
        out_specs=VMEM,
        moved=1 << 20,
    )(cross_got, next_got, core_got, keep)

    def staged(weights):
        return call(
            stage_kernel,
            shaped((4, 1024, HALF), BF16),
            scratch=[pltpu.SemaphoreType.DMA((4,))],
            in_specs=[HBM],
            out_specs=VMEM,
            moved=8 << 20,
            limit=48 * 1024 * 1024,
        )(weights)

    up, down = [normed], [normed]
    for step in range(4):
        if step == 1:
            up[1], weights = lax.optimization_barrier((up[1], weights))
        up.append(lax.ppermute(up[-1], "context", UP))
        if step < 3:
            down.append(lax.ppermute(down[-1], "context", DOWN))
    blocks = {**{r: up[r] for r in range(5)}, **{CHIPS - r: down[r] for r in range(1, 4)}}
    near_weights = staged(weights)
    near = product([blocks[r] for r in NEAR[:-1]], near_weights, len(NEAR))
    near = product([blocks[NEAR[-1]]], near_weights, len(NEAR), len(NEAR) - 1, near)
    blocks[3], weights = lax.optimization_barrier((blocks[3], weights))
    far_weights = staged(weights)
    far = product([blocks[r] for r in FAR[:-1]], far_weights, len(FAR))
    far = product([blocks[FAR[-1]]], far_weights, len(FAR), len(FAR) - 1, far)
    near = lax.psum_scatter(
        near.reshape(4 * 16 * len(NEAR), 1024), "tensor",
        scatter_dimension=0, tiled=True, axis_index_groups=PARITY,
    )
    far = lax.all_to_all(
        far.reshape(4, 16 * len(FAR), 1024), "tensor", 0, 0, tiled=True, axis_index_groups=PARITY
    )
    ready = call(
        collect_kernel,
        shaped((CHIPS, 16, 1024), BF16),
        scratch=[pltpu.VMEM((len(NEAR), 16, 1024), BF16), pltpu.SemaphoreType.DMA((1,))],
        in_specs=[HBM, VMEM],
        moved=2 << 20,
    )(near.reshape(len(NEAR), 16, 1024), far.reshape(4, len(FAR), 16, 1024))
    return lax.all_to_all(
        ready, "context", 0, 0, tiled=True, axis_index_groups=BACKWARD
    )[::-1].transpose(1, 0, 2).reshape(16, 8192)


def solution(mesh):
    return jax.shard_map(
        body,
        mesh=mesh,
        in_specs=(
            P(("dp", "context"), "tensor"),
            P(("dp", "context"), None, "tensor"),
            P(("dp", "context"), "tensor"),
            P(("dp", "context"), "tensor"),
            P("dp", "tensor"),
            P("dp", None, "tensor"),
            P(None, "tensor"),
            P(None, None, "tensor"),
            P("tensor"),
            P("tensor"),
            P("tensor"),
            P(("dp", "tensor"), None, None),
            P("tensor"),
            P("tensor", "context"),
        ),
        out_specs=P(("dp", "context", "tensor"), None),
        check_vma=False,
    )
```
